256 devices in a mesh: energy: 64 (over z_lo, y, x), mom: 2 (over core), tile: 2 (over z_hi).
Axes of the slice: x: 4, y: 4, z: 8 (z_hi: 2, z_lo: 4; z = z_hi * 4 + z_lo), core: 2. Of those that a mesh axis runs over, the one named last changes fastest.
Arguments:
- green: float32 [2, 128, 256, 512], P('mom', ('energy', 'tile')), may hold values from -1.5 to 1.5
- phonon: float32 [256, 256], P(('energy', 'tile')), may hold values from -0.18 to 0.18
- lag_offsets: int32 [32], replicated, may hold values from -32 to 32
- grad_table: float32 [64, 256], replicated, may hold values from -1.5 to 1.5
- neighbor_grad: int32 [256, 4], P(('energy', 'tile')), may hold values from 0 to 63
Outputs:
- sigma: float32 [2, 128, 256, 512], P('mom', ('energy', 'tile'))
- green_next: float32 [2, 128, 256, 512], P('mom', ('energy', 'tile'))
The draws below stay inside these ranges and needn't reach their ends.
All inputs are finite; a program needn't handle non-finite values.
Results may differ from the reference program's by a relative error of at most 0.000078.
Values sent between devices are 32-bit elements; how exact they have to be, the bound alone decides.
A program may use at most 64 MiB of HBM per device.

```python
import jax
import jax.numpy as jnp
from jax import lax

NO = 16
NBR = 4
LAGS = 32
NGRAD = 64
MOMENTA = 2
NE = 128
NA = 256
LAGSPAN = 32


def with_ends(values, own_key, least, largest):
    longest = values.shape.index(max(values.shape))
    spots = []
    for shift in (0, 1):
        where = [jax.random.randint(jax.random.fold_in(own_key, axis), (), 0, length) for axis, length in enumerate(values.shape)]
        where[longest] = (where[longest] + shift) % values.shape[longest]
        spots.append(tuple(where))
    return values.at[spots[0]].set(least).at[spots[1]].set(largest)


def steps_of(rng, shape, cuts, low, largest):
    def one(dim, shards_of):
        steps = jax.random.uniform(jax.random.fold_in(jax.random.fold_in(rng, 6), dim), (shards_of,), jnp.float32, low / len(cuts), largest / len(cuts))
        return jnp.repeat(jnp.exp(steps), shape[dim] // shards_of).reshape((-1,) + (1,) * (len(shape) - dim - 1))

    loudness = one(*cuts[0])
    for cut in cuts[1:]:
        loudness = loudness * one(*cut)
    return loudness


def scatter_about(stream_key, shape, spread, bound, split=(), held_as=jnp.bfloat16):
    drawn = jax.random.normal(stream_key, shape, jnp.float32) * spread
    if len(split) > 0:
        drawn = steps_of(stream_key, shape, split, -0.22, 0.18) * drawn
    return jnp.clip(drawn, min=-bound, max=bound).astype(held_as)


def setup_inputs(seed: int = 0) -> dict:
    streams_of = jax.random.split(jax.random.key(seed), 6)
    green = scatter_about(streams_of[0], (MOMENTA, NE, NA, 2 * NO * NO), 0.25, 1.5, ((0, 2), (1, 128)), jnp.float32)
    phonon = scatter_about(streams_of[1], (NA, 2 * LAGS * NBR), 0.03, 0.18, ((0, 128),), jnp.float32)
    lag_offsets = with_ends(jax.random.randint(streams_of[2], (LAGS,), -LAGSPAN, LAGSPAN + 1), jax.random.fold_in(streams_of[2], 1), -LAGSPAN, LAGSPAN).astype(jnp.int32)
    grad_table = scatter_about(streams_of[3], (NGRAD, NO * NO), NO ** -0.5, 1.5, (), jnp.float32)
    neighbor_grad = with_ends(jax.random.randint(streams_of[4], (NA, NBR), 0, NGRAD), jax.random.fold_in(streams_of[4], 1), 0, NGRAD - 1).astype(jnp.int32)
    return dict(green=green, phonon=phonon, lag_offsets=lag_offsets, grad_table=grad_table, neighbor_grad=neighbor_grad)


PRECISE = lax.Precision.HIGHEST


def batch_product(left, right):
    return jnp.einsum("...ij,...jk->...ik", left, right, precision=PRECISE)


def complex_product(left, right):
    left_real, left_imag = left[..., 0, :, :], left[..., 1, :, :]
    right_real, right_imag = right[..., 0, :, :], right[..., 1, :, :]
    real_part = batch_product(left_real, right_real) - batch_product(left_imag, right_imag)
    imag_part = batch_product(left_real, right_imag) + batch_product(left_imag, right_real)
    return jnp.stack([real_part, imag_part], axis=-3)


def dyson(green_blocks, sigma_blocks):
    extent = green_blocks.shape
    green_split = green_blocks.reshape(extent[:-1] + (2, NO, NO))
    sigma_split = sigma_blocks.reshape(extent[:-1] + (2, NO, NO))
    product = complex_product(green_split, sigma_split)
    second = green_split + complex_product(product, green_split)
    return (green_split + complex_product(product, second)).reshape(extent)


def atom_sigma(item, lag_offsets, grad_table):
    green_atom, coeff_row, index_row = item
    coeffs = coeff_row.reshape(2, LAGS, NBR)
    diffs = jnp.arange(2 * NE - 1, dtype=jnp.int32) - (NE - 1)
    selector = (lag_offsets[:, None] == diffs[None, :]).astype(coeff_row.dtype)
    profile = jnp.einsum("qln,ld->nqd", coeffs, selector, precision=PRECISE)
    energy_index = jnp.arange(NE, dtype=jnp.int32)
    position = energy_index[:, None] - energy_index[None, :] + (NE - 1)
    matrices = profile[:, :, position]
    gradients = grad_table[index_row].reshape(NBR, NO, NO)
    halves = green_atom.reshape(2, NE, 2, NO, NO)
    sandwiched = jnp.einsum("nij,kecjl,nml->knecim", gradients, halves, gradients, precision=PRECISE)
    sandwiched = sandwiched.reshape(2, NBR, NE, 2 * NO * NO)
    first = jnp.einsum("nqij,qnjc->ic", matrices, sandwiched, precision=PRECISE)
    second = jnp.einsum("nqij,qnjc->ic", matrices, sandwiched[::-1], precision=PRECISE)
    return jnp.stack([first, second], axis=0)


def reference(green, phonon, lag_offsets, grad_table, neighbor_grad):
    by_atom = jnp.moveaxis(green, 2, 0)
    sigma_atoms = lax.map(lambda item: atom_sigma(item, lag_offsets, grad_table), (by_atom, phonon, neighbor_grad))
    sigma = jnp.moveaxis(sigma_atoms, 0, 2)
    green_next = dyson(green, sigma)
    return sigma, green_next
```

```python
import functools

import jax
import jax.numpy as jnp
from jax import lax
from jax.experimental import pallas as pl
from jax.experimental.pallas import tpu as pltpu
from jax.sharding import PartitionSpec as P

MESH = pl.DeviceIdType.MESH
EXACT = lax.Precision.HIGHEST
F32, BF16 = jnp.float32, jnp.bfloat16
NE = 128
PAIRS = 128
NBR = 4


def split(value):
    high = value.astype(BF16)
    return high, (value - high.astype(F32)).astype(BF16)


def iota(shape, dim):
    return lax.broadcasted_iota(jnp.int32, shape, dim)


def coordinates():
    energy = lax.axis_index("energy")
    return (
        energy // 16 + 4 * lax.axis_index("tile"),
        (energy // 4) % 4,
        energy % 4,
        lax.axis_index("mom"),
    )


def device_at(z, y, x):
    return {"energy": (z % 4) * 16 + y * 4 + x, "tile": z // 4}


def flat_at(z, y, x):
    return ((z % 4) * 16 + y * 4 + x) * 2 + z // 4


def lines(z, y, x):
    along_z = [device_at((z + step) % 8, y, x) for step in range(1, 8)]
    along_y = [device_at(z, (y + step) % 4, x) for step in range(1, 4)]
    along_x = [device_at(z, y, (x + step) % 4) for step in range(1, 4)]
    return along_z, along_y, along_x


def signal(sem, device):
    pl.semaphore_signal(sem, inc=1, device_id=device, device_id_type=MESH)


def tile_rows(block):
    return pl.ds(pl.multiple_of(block * 8, 8), 8)


def exchange_start(position, source, landing, send_sem, recv_sem, shift_target):
    z, y, x = position
    here = tile_rows(flat_at(z, y, x))
    depth = [((z + step) % 8) for step in range(8)]

    def send(zz, yy, xx):
        pltpu.make_async_remote_copy(
            src_ref=source.at[tile_rows(flat_at(zz, yy, xx))],
            dst_ref=landing.at[here],
            send_sem=send_sem,
            recv_sem=recv_sem,
            device_id=device_at(zz, yy, xx),
            device_id_type=MESH,
        ).start()

    for zz in depth[1:]:
        send(zz, y, x)

    @pl.loop(1, 16)
    def _(k):
        yy = (y + k // 4) % 4
        xx = (x + k % 4) % 4
        for zz in depth:
            send(zz, yy, xx)

    landing[here, :] = source[here, :]


def exchange_descriptor(source, landing, send_sem, recv_sem, device):
    rows = pl.ds(0, 8 * 127)
    return pltpu.make_async_remote_copy(
        src_ref=source.at[rows],
        dst_ref=landing.at[rows],
        send_sem=send_sem,
        recv_sem=recv_sem,
        device_id=device,
        device_id_type=MESH,
    )


def build_weights(core, phonon, lags, whi, wlo):
    place = (iota((256, 32), 0) // 4) % 32 == iota((256, 32), 1)
    lag_column = jnp.sum(
        jnp.where(place, jnp.broadcast_to(lags[...], (256, 32)), 0), axis=1, keepdims=True
    )
    lane = iota((256, 256), 1)
    offset = jnp.where(lane < 128, lane, lane - 256)
    picked = jnp.where(offset == -lag_column, 1.0, 0.0).astype(F32)
    row, column = iota((8, 256), 0), iota((8, 256), 1)
    mine = (column // 128 == row // 4) & (column % 4 == row % 4)
    coeffs = jnp.where(mine, jnp.broadcast_to(phonon[pl.ds(core, 1), :], (8, 256)), 0.0)
    profile = jnp.dot(coeffs, picked, precision=EXACT, preferred_element_type=F32)
    for q in range(2):
        for n in range(NBR):
            spread = jnp.broadcast_to(profile[q * 4 + n : q * 4 + n + 1, :], (128, 256))
            toeplitz = pltpu.roll(spread, 0, 1, stride=1, stride_axis=0)[:, :128]
            high, low = split(toeplitz)
            for k in range(2):
                rows = slice(n * 256 + k * 128, n * 256 + k * 128 + 128)
                cols = slice(((k + q) % 2) * 128, ((k + q) % 2) * 128 + 128)
                whi[rows, cols] = high
                wlo[rows, cols] = low


def build_kron(core, neighbor, grad, khi, klo, factors):
    column = iota((16, 256), 1)
    mine = column % 16 == iota((16, 256), 0)
    source, target = iota((256, 256), 0), iota((256, 256), 1)
    outer = jnp.where(source // 16 == target // 16, 1.0, 0.0).astype(F32)
    inner = jnp.where(source // 16 == target % 16, 1.0, 0.0).astype(F32)
    for n in range(NBR):
        block = jnp.broadcast_to(grad[pl.ds(neighbor[core, n], 1), :], (16, 256))
        factors[n * 16 : n * 16 + 16, :] = jnp.where(mine, block, 0.0)
    left = factors[...]
    first = jnp.dot(left, outer, precision=EXACT, preferred_element_type=F32)
    second = jnp.dot(left, inner, precision=EXACT, preferred_element_type=F32)
    for n in range(NBR):
        for j in range(16):
            row = first[n * 16 + j : n * 16 + j + 1, :]
            high, low = split(row * second[n * 16 : n * 16 + 16, :])
            rows = slice(n * 256 + j * 16, n * 256 + j * 16 + 16)
            khi[rows, :] = high
            klo[rows, :] = low


def contract(got, xhi, xlo, whi, wlo, khi, klo, hhi, hlo, result):
    for k in range(2):
        for t in range(4):
            high, low = split(got[pl.ds(k * 4 + t, NE, stride=8), :])
            rows, cols = slice(k * 128, k * 128 + 128), slice(t * 128, t * 128 + 128)
            xhi[rows, cols] = high
            xlo[rows, cols] = low
    high, low = xhi[...], xlo[...]
    right = jnp.concatenate([high, low, high], axis=0)

    @pl.loop(0, NBR)
    def _(n):
        rows = pl.ds(pl.multiple_of(n * 256, 256), 256)
        wh, wl = whi[rows, :], wlo[rows, :]
        mixed = jnp.dot(
            jnp.concatenate([wh, wh, wl], axis=1), right, preferred_element_type=F32
        )
        high, low = split(mixed)
        hhi[n] = high
        hlo[n] = low

    for part in range(2):
        cols = slice(part * 256, part * 256 + 256)
        total = None
        for n in range(NBR):
            rows = slice(n * 256, n * 256 + 256)
            kh, kl = khi[rows, :], klo[rows, :]
            hh, hl = hhi[n, :, cols], hlo[n, :, cols]
            term = jnp.dot(
                jnp.concatenate([hh, hh, hl], axis=1),
                jnp.concatenate([kh, kl, kh], axis=0),
                preferred_element_type=F32,
            )
            total = term if total is None else total + term
        for k in range(2):
            for half in range(2):
                result[pl.ds(k * 4 + part * 2 + half, NE, stride=8), :] = total[
                    k * 128 : k * 128 + 128, half * 128 : half * 128 + 128
                ]


def load_columns(source, target, sems):
    loads = [
        pltpu.make_async_copy(
            source.at[:, pl.ds(t * 128, 128)], target.at[pl.ds(t * 256, 256)], sems.at[t]
        )
        for t in range(4)
    ]
    for load in loads:
        load.start()
    return loads


def scatter_kernel(
    green, phonon, lags, grad, neighbor, sigma,
    held, swap_out, swap_in, stage, got, result, back, whi, wlo, khi, klo, factors, xhi, xlo, hhi, hlo,
    send_sems, recv_sems, stage_sems, load_sem,
):
    loads = load_columns(green, held, load_sem)
    z, y, x, core = coordinates()
    position = (z, y, x)
    sibling = {"mom": 1 - core}
    along_z, along_y, along_x = lines(z, y, x)
    barrier = pltpu.get_barrier_semaphore()
    for device in [sibling] + along_z + along_y + along_x:
        signal(barrier, device)

    for load in loads:
        load.wait()
    for t in range(4):
        swap_out[t] = held[pl.ds(t * 256 + 1 - core, PAIRS, stride=2), :]
        stage[pl.ds(core * 4 + t, PAIRS, stride=8), :] = held[
            pl.ds(t * 256 + core, PAIRS, stride=2), :
        ]
    pl.semaphore_wait(barrier, 14)

    swap = pltpu.make_async_remote_copy(
        src_ref=swap_out, dst_ref=swap_in, send_sem=send_sems.at[0], recv_sem=recv_sems.at[0],
        device_id=sibling, device_id_type=MESH,
    )
    swap.start()
    for device in along_y:
        signal(stage_sems.at[0], device)
    build_weights(core, phonon, lags, whi, wlo)
    pl.semaphore_wait(stage_sems.at[0], 3)
    for device in along_x:
        signal(stage_sems.at[1], device)
    swap.wait()
    for t in range(4):
        stage[pl.ds((1 - core) * 4 + t, PAIRS, stride=8), :] = swap_in[t]
    pl.semaphore_wait(stage_sems.at[1], 3)

    exchange_start(position, stage, got, send_sems.at[1], recv_sems.at[1], None)
    build_kron(core, neighbor, grad, khi, klo, factors)
    exchange_descriptor(stage, got, send_sems.at[1], recv_sems.at[1], sibling).wait()
    contract(got, xhi, xlo, whi, wlo, khi, klo, hhi, hlo, result)
    exchange_start(position, result, back, send_sems.at[2], recv_sems.at[2], None)
    exchange_descriptor(result, back, send_sems.at[2], recv_sems.at[2], sibling).wait()

    for t in range(4):
        swap_out[t] = back[pl.ds((1 - core) * 4 + t, PAIRS, stride=8), :]
    swap_back = pltpu.make_async_remote_copy(
        src_ref=swap_out, dst_ref=sigma.at[1], send_sem=send_sems.at[3], recv_sem=recv_sems.at[3],
        device_id=sibling, device_id_type=MESH,
    )
    swap_back.start()
    for t in range(4):
        sigma[0, t] = back[pl.ds(core * 4 + t, PAIRS, stride=8), :]
    swap_back.wait()


def scatter(green, phonon, lags, grad, neighbor):
    vmem = pl.BlockSpec(memory_space=pltpu.VMEM)
    return pl.pallas_call(
        scatter_kernel,
        out_shape=jax.ShapeDtypeStruct((2, 4, PAIRS, 128), F32),
        in_specs=[pl.BlockSpec(memory_space=pl.ANY)] + [vmem] * 3 + [pl.BlockSpec(memory_space=pltpu.SMEM)],
        out_specs=vmem,
        scratch_shapes=[
            pltpu.VMEM((1024, 128), F32),
            pltpu.VMEM((4, PAIRS, 128), F32),
            pltpu.VMEM((4, PAIRS, 128), F32),
            pltpu.VMEM((1024, 128), F32),
            pltpu.VMEM((1024, 128), F32),
            pltpu.VMEM((1024, 128), F32),
            pltpu.VMEM((1024, 128), F32),
            pltpu.VMEM((1024, 256), BF16),
            pltpu.VMEM((1024, 256), BF16),
            pltpu.VMEM((1024, 256), BF16),
            pltpu.VMEM((1024, 256), BF16),
            pltpu.VMEM((64, 256), F32),
            pltpu.VMEM((256, 512), BF16),
            pltpu.VMEM((256, 512), BF16),
            pltpu.VMEM((NBR, 256, 512), BF16),
            pltpu.VMEM((NBR, 256, 512), BF16),
            pltpu.SemaphoreType.DMA((4,)),
            pltpu.SemaphoreType.DMA((4,)),
            pltpu.SemaphoreType.REGULAR((2,)),
            pltpu.SemaphoreType.DMA((4,)),
        ],
        compiler_params=pltpu.CompilerParams(
            collective_id=0, has_side_effects=True, vmem_limit_bytes=40 * 1024 * 1024
        ),
        cost_estimate=pl.CostEstimate(
            flops=2 * 10**9, bytes_accessed=4 * 10**6, transcendentals=0
        ),
    )(green, phonon, lags, grad, neighbor)


def complex_rows(target, left, right, base):
    @pl.loop(0, 4)
    def _(block):
        first = pl.multiple_of(block * 64, 64)
        real = [None] * 4
        imag = [None] * 4
        for j in range(16):
            b_real = right[j * 16 : j * 16 + 16, :]
            b_imag = right[256 + j * 16 : 256 + j * 16 + 16, :]
            for i in range(4):
                a_real = left[pl.ds(first + i * 16 + j, 1), :]
                a_imag = left[pl.ds(256 + first + i * 16 + j, 1), :]
                add_real = a_real * b_real - a_imag * b_imag
                add_imag = a_real * b_imag + a_imag * b_real
                real[i] = add_real if j == 0 else real[i] + add_real
                imag[i] = add_imag if j == 0 else imag[i] + add_imag
        for i in range(4):
            rows = pl.ds(first + i * 16, 16)
            late = pl.ds(256 + first + i * 16, 16)
            if base is None:
                target[rows, :] = real[i]
                target[late, :] = imag[i]
            else:
                target[rows, :] = base[rows, :] + real[i]
                target[late, :] = base[late, :] + imag[i]


def store_columns(source, target, sems):
    stores = [
        pltpu.make_async_copy(
            source.at[pl.ds(t * 256, 256)], target.at[:, pl.ds(t * 128, 128)], sems.at[t]
        )
        for t in range(4)
    ]
    for store in stores:
        store.start()
    return stores


def dyson_kernel(
    green, blocks, sigma, after, held, summed, final, g_rows, s_rows, r_rows, x_rows,
    load_sem, sigma_sem, after_sem,
):
    core = lax.axis_index("mom")
    loads = load_columns(green, held, load_sem)
    for which in range(2):
        parity = core if which == 0 else 1 - core
        for t in range(4):
            summed[pl.ds(t * 256 + parity, PAIRS, stride=2), :] = blocks[which, t]
    stores = store_columns(summed, sigma, sigma_sem)
    for load in loads:
        load.wait()

    @pl.loop(0, 2)
    def _(parity):
        for t in range(4):
            rows = slice(t * 128, t * 128 + 128)
            atoms = pl.ds(t * 256 + parity, PAIRS, stride=2)
            s_rows[rows, :] = summed[atoms, :].T
            g_rows[rows, :] = held[atoms, :].T
        complex_rows(r_rows, g_rows, s_rows, None)
        complex_rows(x_rows, r_rows, g_rows, g_rows)
        complex_rows(s_rows, r_rows, x_rows, g_rows)
        for t in range(4):
            rows = slice(t * 128, t * 128 + 128)
            final[pl.ds(t * 256 + parity, PAIRS, stride=2), :] = s_rows[rows, :].T

    stores += store_columns(final, after, after_sem)
    for store in stores:
        store.wait()


def dyson(green, blocks):
    whole = pl.BlockSpec(memory_space=pl.ANY)
    return pl.pallas_call(
        dyson_kernel,
        out_shape=[jax.ShapeDtypeStruct((256, 512), F32)] * 2,
        in_specs=[whole, pl.BlockSpec(memory_space=pltpu.VMEM)],
        out_specs=[whole] * 2,
        scratch_shapes=[pltpu.VMEM((1024, 128), F32)] * 3
        + [pltpu.VMEM((512, 128), F32)] * 4
        + [pltpu.SemaphoreType.DMA((4,))] * 3,
        compiler_params=pltpu.CompilerParams(vmem_limit_bytes=16 * 1024 * 1024),
        cost_estimate=pl.CostEstimate(
            flops=3 * 10**7, bytes_accessed=2 * 10**6, transcendentals=0
        ),
    )(green, blocks)


def body(green, phonon, lag_offsets, grad_table, neighbor_grad):
    own = green.reshape(256, 512)
    blocks = scatter(own, phonon, lag_offsets.reshape(1, 32), grad_table, neighbor_grad)
    sigma, after = dyson(own, blocks)
    return sigma.reshape(green.shape), after.reshape(green.shape)


def solution(mesh):
    whole = P("mom", ("energy", "tile"), None, None)
    rows = P(("energy", "tile"), None)
    return jax.shard_map(
        body,
        mesh=mesh,
        in_specs=(whole, rows, P(), P(), rows),
        out_specs=(whole, whole),
        check_vma=False,
    )
```

```python
import functools

import jax
import jax.numpy as jnp
from jax import lax
from jax.experimental import pallas as pl
from jax.experimental.pallas import tpu as pltpu
from jax.sharding import PartitionSpec as P

MESH = pl.DeviceIdType.MESH
EXACT = lax.Precision.HIGHEST
F32, BF16 = jnp.float32, jnp.bfloat16
NE = 128
PAIRS = 128
NBR = 4


def split(value):
    high = value.astype(BF16)
    return high, (value - high.astype(F32)).astype(BF16)


def iota(shape, dim):
    return lax.broadcasted_iota(jnp.int32, shape, dim)


def coordinates():
    energy = lax.axis_index("energy")
    return (
        energy // 16 + 4 * lax.axis_index("tile"),
        (energy // 4) % 4,
        energy % 4,
        lax.axis_index("mom"),
    )


def device_at(z, y, x):
    return {"energy": (z % 4) * 16 + y * 4 + x, "tile": z // 4}


def flat_at(z, y, x):
    return ((z % 4) * 16 + y * 4 + x) * 2 + z // 4


def neighbours(z, y, x):
    column = [device_at((z + step) % 8, y, x) for step in range(1, 8)]
    plane = [device_at(z, (y + step // 4) % 4, (x + step % 4) % 4) for step in range(1, 16)]
    return column, plane


def signal(sem, device):
    pl.semaphore_signal(sem, inc=1, device_id=device, device_id_type=MESH)


def tile_rows(block):
    return pl.ds(pl.multiple_of(block * 8, 8), 8)


def exchange_start(position, half, source, landing, send_sem, recv_sem):
    z, y, x = position
    here = tile_rows(flat_at(z, y, x))
    depth = [(z + step) % 8 for step in (0, 4, 3, 5, 2, 6, 1, 7)]

    def send(zz, yy, xx):
        pltpu.make_async_remote_copy(
            src_ref=source.at[tile_rows(flat_at(zz, yy, xx))],
            dst_ref=landing.at[here],
            send_sem=send_sem,
            recv_sem=recv_sem,
            device_id=device_at(zz, yy, xx),
            device_id_type=MESH,
        ).start()

    if half == 0:
        for zz in depth[1:]:
            send(zz, y, x)

    @pl.loop(1 - half, 8)
    def _(k):
        yy = (y + k // 2) % 4
        xx = (x + half + 2 * (k % 2)) % 4
        for zz in depth:
            send(zz, yy, xx)

    if half == 0:
        landing[here, :] = source[here, :]


def exchange_descriptor(half, source, landing, send_sem, recv_sem, device):
    rows = pl.ds(0, 8 * (63 + half))
    return pltpu.make_async_remote_copy(
        src_ref=source.at[rows],
        dst_ref=landing.at[rows],
        send_sem=send_sem,
        recv_sem=recv_sem,
        device_id=device,
        device_id_type=MESH,
    )


def build_weights(core, phonon, lags, whi, wlo):
    place = (iota((256, 32), 0) // 4) % 32 == iota((256, 32), 1)
    lag_column = jnp.sum(
        jnp.where(place, jnp.broadcast_to(lags[...], (256, 32)), 0), axis=1, keepdims=True
    )
    lane = iota((256, 256), 1)
    offset = jnp.where(lane < 128, lane, lane - 256)
    picked = jnp.where(offset == -lag_column, 1.0, 0.0).astype(F32)
    row, column = iota((8, 256), 0), iota((8, 256), 1)
    mine = (column // 128 == row // 4) & (column % 4 == row % 4)
    coeffs = jnp.where(mine, jnp.broadcast_to(phonon[pl.ds(core, 1), :], (8, 256)), 0.0)
    profile = jnp.dot(coeffs, picked, precision=EXACT, preferred_element_type=F32)
    source, target = iota((256, 256), 0), iota((256, 256), 1)
    energy = 4 * (target % 32) + 2 * (target // 128) + (target // 32) % 2
    orders = [
        jnp.where(
            (source % 128 == energy) & (source // 128 == (target // 64 + k) % 2), 1.0, 0.0
        ).astype(BF16)
        for k in range(2)
    ]
    for n in range(NBR):
        parts = [
            jnp.concatenate(
                [
                    pltpu.roll(
                        jnp.broadcast_to(profile[q * 4 + n : q * 4 + n + 1, :], (32, 256)),
                        step,
                        1,
                        stride=4,
                        stride_axis=0,
                    )[:, :128]
                    for q in range(2)
                ],
                axis=1,
            )
            for step in range(4)
        ]
        pieces = split(jnp.concatenate(parts, axis=0))
        for piece, kept in zip(pieces, (whi, wlo)):
            for k in range(2):
                moved = jnp.dot(piece, orders[k], preferred_element_type=F32).astype(BF16)
                for s in range(2):
                    rows = slice(s * 128 + k * 64, s * 128 + k * 64 + 64)
                    for other in range(2):
                        kept[other, rows, n * 128 : n * 128 + 128] = moved[
                            s * 64 : s * 64 + 64, other * 128 : other * 128 + 128
                        ]


def build_kron(core, neighbor, grad, khi, klo, factors):
    column = iota((16, 256), 1)
    mine = column % 16 == iota((16, 256), 0)
    source, target = iota((256, 256), 0), iota((256, 256), 1)
    outer = jnp.where(source // 16 == target // 16, 1.0, 0.0).astype(F32)
    inner = jnp.where(source // 16 == target % 16, 1.0, 0.0).astype(F32)
    for n in range(NBR):
        block = jnp.broadcast_to(grad[pl.ds(neighbor[core, n], 1), :], (16, 256))
        factors[n * 16 : n * 16 + 16, :] = jnp.where(mine, block, 0.0)
    left = factors[...]
    first = jnp.dot(left, outer, precision=EXACT, preferred_element_type=F32)
    second = jnp.dot(left, inner, precision=EXACT, preferred_element_type=F32)
    for n in range(NBR):
        for j in range(16):
            row = first[n * 16 + j : n * 16 + j + 1, :]
            high, low = split(row * second[n * 16 : n * 16 + 16, :])
            rows = slice(n * 256 + j * 16, n * 256 + j * 16 + 16)
            khi[rows, :] = high
            klo[rows, :] = low


def three_passes(left, right):
    lh, ll = left
    rh, rl = right
    return jnp.dot(
        jnp.concatenate([lh, lh, ll], axis=1),
        jnp.concatenate([rh, rl, rh], axis=0),
        preferred_element_type=F32,
    )


def energy_rows(s, zh, k, t):
    return pl.ds(16 * s + 8 * zh + 4 * k + t, 32, stride=32)


def sandwich_half(s, got, khi, klo, fhi, flo):
    loaded = [
        jnp.concatenate(
            [
                jnp.concatenate(
                    [got[energy_rows(s, zh, k, 2 * part + side), :] for side in range(2)], axis=1
                )
                for k in range(2)
                for zh in range(2)
            ],
            axis=0,
        )
        for part in range(2)
    ]
    left = split(jnp.concatenate(loaded, axis=0))
    for n in range(NBR):
        rows = slice(n * 256, n * 256 + 256)
        high, low = split(three_passes(left, (khi[rows, :], klo[rows, :])))
        for part in range(2):
            to, cols = slice(n * 128, n * 128 + 128), slice(part * 256, part * 256 + 256)
            fhi[to, cols] = high[part * 128 : part * 128 + 128, :]
            flo[to, cols] = low[part * 128 : part * 128 + 128, :]


def mix_half(rows, s, whi, wlo, fhi, flo):
    return three_passes((whi[s, rows, :], wlo[s, rows, :]), (fhi[...], flo[...]))


def load_columns(source, target, sems):
    loads = [
        pltpu.make_async_copy(
            source.at[:, pl.ds(t * 128, 128)], target.at[pl.ds(t * 256, 256)], sems.at[t]
        )
        for t in range(4)
    ]
    for load in loads:
        load.start()
    return loads


def atom_rows(t, s, zh, parity):
    return pl.ds(t * 256 + 4 * s + 2 * zh + parity, 32, stride=8)


def block_rows(t, zh, parity):
    return pl.ds(pl.multiple_of(t * 128 + zh * 64 + parity * 32, 32), 32)


QUARTERS = [(t, zh, parity) for t in range(4) for zh in range(2) for parity in range(2)]


def pick_half(source, target, s):
    for t, zh, parity in QUARTERS:
        target[block_rows(t, zh, parity), :] = source[atom_rows(t, s, zh, parity), :]


def place_half(source, target, s):
    for t, zh, parity in QUARTERS:
        target[atom_rows(t, s, zh, parity), :] = source[block_rows(t, zh, parity), :]


def turn(source, target):
    for t in range(4):
        rows = slice(t * 128, t * 128 + 128)
        target[rows, :] = source[rows, :].T


def dyson_rows(g_rows, s_rows, r_rows, x_rows):
    complex_rows(r_rows, g_rows, s_rows, None)
    complex_rows(x_rows, r_rows, g_rows, g_rows)
    complex_rows(s_rows, r_rows, x_rows, g_rows)


def scatter_kernel(
    green, phonon_in, lags_in, grad_in, neighbor_in, kept,
    held, phonon, lags, grad, neighbor,
    swap_out, swap_in, late_out, late_in, stage, got, result, back,
    whi, wlo, khi, klo, factors, fhi, flo, partial, summed, early, g_rows, s_rows, r_rows, x_rows,
    send_sems, recv_sems, stage_sem, load_sem, small_sem, keep_sem,
):
    z, y, x, core = coordinates()
    position = (z, y, x)
    parities = (x % 2, 1 - x % 2)
    sibling = {"mom": 1 - core}
    column, plane = neighbours(z, y, x)
    barrier = pltpu.get_barrier_semaphore()
    for device in [sibling] + plane + column:
        signal(barrier, device)
    loads = load_columns(green, held, load_sem)
    smalls = [
        pltpu.make_async_copy(source, target, small_sem.at[i])
        for i, (source, target) in enumerate(
            [(phonon_in, phonon), (lags_in, lags), (grad_in, grad), (neighbor_in, neighbor)]
        )
    ]
    for small in smalls:
        small.start()

    def channel(i):
        return send_sems.at[i], recv_sems.at[i]

    def swap_of(half, source, target, i):
        return pltpu.make_async_remote_copy(
            src_ref=source.at[half],
            dst_ref=target.at[half],
            send_sem=send_sems.at[i + half],
            recv_sem=recv_sems.at[i + half],
            device_id=sibling,
            device_id_type=MESH,
        )

    for load in loads:
        load.wait()
    for half, s in enumerate(parities):
        for zh in range(2):
            for t in range(4):
                swap_out[half, zh * 4 + t] = held[atom_rows(t, s, zh, 1 - core), :]
    pl.semaphore_wait(barrier, 23)

    swaps = [swap_of(half, swap_out, swap_in, 0) for half in range(2)]
    for swap in swaps:
        swap.start()
    for device in column:
        signal(stage_sem, device)
    for t in range(4):
        stage[pl.ds(core * 4 + t, PAIRS, stride=8), :] = held[
            pl.ds(t * 256 + core, PAIRS, stride=2), :
        ]
    pl.semaphore_wait(stage_sem, 7)
    for half, s in enumerate(parities):
        swaps[half].wait()
        for zh in range(2):
            for t in range(4):
                stage[energy_rows(s, zh, 1 - core, t), :] = swap_in[half, zh * 4 + t]
        exchange_start(position, half, stage, got, *channel(2 + half))

    for small in smalls:
        small.wait()
    build_weights(core, phonon, lags, whi, wlo)
    build_kron(core, neighbor, grad, khi, klo, factors)

    def keep(i, source):
        copy = pltpu.make_async_copy(source, kept.at[i], keep_sem.at[i])
        copy.start()
        return copy

    pick_half(held, r_rows, parities[1])
    turn(r_rows, x_rows)
    keeps = [keep(0, x_rows)]
    pick_half(held, s_rows, parities[0])
    turn(s_rows, g_rows)

    exchange_descriptor(0, stage, got, *channel(2), sibling).wait()
    sandwich_half(parities[0], got, khi, klo, fhi, flo)
    for out in range(2):
        rows = slice(out * 128, out * 128 + 128)
        partial[rows, :] = mix_half(rows, parities[0], whi, wlo, fhi, flo)
    exchange_descriptor(1, stage, got, *channel(3), sibling).wait()
    sandwich_half(parities[1], got, khi, klo, fhi, flo)
    for half, s in enumerate(parities):
        rows = pl.ds(pl.multiple_of(s * 128, 128), 128)
        total = partial[rows, :] + mix_half(rows, parities[1], whi, wlo, fhi, flo)
        for k in range(2):
            for zh in range(2):
                first = k * 64 + zh * 32
                for t in range(4):
                    result[energy_rows(s, zh, k, t), :] = total[
                        first : first + 32, t * 128 : t * 128 + 128
                    ]
        exchange_start(position, half, result, back, *channel(4 + half))

    keeps[0].wait()
    for half, s in enumerate(parities):
        exchange_descriptor(half, result, back, *channel(4 + half), sibling).wait()
        for zh in range(2):
            for t in range(4):
                late_out[half, zh * 4 + t] = back[energy_rows(s, zh, 1 - core, t), :]
        swap_back = swap_of(half, late_out, late_in, 6)
        swap_back.start()
        for zh in range(2):
            for t in range(4):
                summed[half, block_rows(t, zh, core), :] = back[energy_rows(s, zh, core, t), :]
        swap_back.wait()
        for zh in range(2):
            for t in range(4):
                summed[half, block_rows(t, zh, 1 - core), :] = late_in[half, zh * 4 + t]
        keeps.append(keep(1 + half, summed.at[half]))
        if half == 0:
            turn(summed.at[0], s_rows)
            dyson_rows(g_rows, s_rows, r_rows, x_rows)
            turn(s_rows, early)
            keeps.append(keep(3, early))
    for copy in keeps[1:]:
        copy.wait()


def scatter(green, phonon, lags, grad, neighbor):
    column = pltpu.VMEM((1024, 128), F32)
    half = pltpu.VMEM((512, 128), F32)
    swapped = pltpu.VMEM((2, 8, 32, 128), F32)
    return pl.pallas_call(
        scatter_kernel,
        out_shape=jax.ShapeDtypeStruct((4, 512, 128), F32),
        in_specs=[pl.BlockSpec(memory_space=pltpu.HBM)] * 5,
        out_specs=pl.BlockSpec(memory_space=pltpu.HBM),
        scratch_shapes=[
            column,
            pltpu.VMEM((2, 256), F32),
            pltpu.VMEM((1, 32), jnp.int32),
            pltpu.VMEM((64, 256), F32),
            pltpu.SMEM((2, 4), jnp.int32),
            swapped,
            swapped,
            swapped,
            swapped,
            column,
            column,
            column,
            column,
            pltpu.VMEM((2, 256, 512), BF16),
            pltpu.VMEM((2, 256, 512), BF16),
            pltpu.VMEM((1024, 256), BF16),
            pltpu.VMEM((1024, 256), BF16),
            pltpu.VMEM((64, 256), F32),
            pltpu.VMEM((512, 512), BF16),
            pltpu.VMEM((512, 512), BF16),
            pltpu.VMEM((256, 512), F32),
            pltpu.VMEM((2, 512, 128), F32),
            half,
            half,
            half,
            half,
            half,
            pltpu.SemaphoreType.DMA((8,)),
            pltpu.SemaphoreType.DMA((8,)),
            pltpu.SemaphoreType.REGULAR,
            pltpu.SemaphoreType.DMA((4,)),
            pltpu.SemaphoreType.DMA((4,)),
            pltpu.SemaphoreType.DMA((4,)),
        ],
        compiler_params=pltpu.CompilerParams(
            collective_id=0, has_side_effects=True, vmem_limit_bytes=56 * 1024 * 1024
        ),
        cost_estimate=pl.CostEstimate(
            flops=2 * 10**9, bytes_accessed=4 * 10**6, transcendentals=0
        ),
    )(green, phonon, lags, grad, neighbor)


def complex_rows(target, left, right, base):
    @pl.loop(0, 4)
    def _(block):
        first = pl.multiple_of(block * 64, 64)
        real = [None] * 4
        imag = [None] * 4
        for j in range(16):
            b_real = right[j * 16 : j * 16 + 16, :]
            b_imag = right[256 + j * 16 : 256 + j * 16 + 16, :]
            for i in range(4):
                a_real = left[pl.ds(first + i * 16 + j, 1), :]
                a_imag = left[pl.ds(256 + first + i * 16 + j, 1), :]
                add_real = a_real * b_real - a_imag * b_imag
                add_imag = a_real * b_imag + a_imag * b_real
                real[i] = add_real if j == 0 else real[i] + add_real
                imag[i] = add_imag if j == 0 else imag[i] + add_imag
        for i in range(4):
            rows = pl.ds(first + i * 16, 16)
            late = pl.ds(256 + first + i * 16, 16)
            if base is None:
                target[rows, :] = real[i]
                target[late, :] = imag[i]
            else:
                target[rows, :] = base[rows, :] + real[i]
                target[late, :] = base[late, :] + imag[i]


def store_columns(source, target, sems):
    stores = [
        pltpu.make_async_copy(
            source.at[pl.ds(t * 256, 256)], target.at[:, pl.ds(t * 128, 128)], sems.at[t]
        )
        for t in range(4)
    ]
    for store in stores:
        store.start()
    return stores


def dyson_kernel(
    kept, sigma, after, held, turned, summed, final, s_rows, r_rows, x_rows,
    load_sem, sigma_sem, after_sem,
):
    soon = lax.axis_index("energy") % 2
    loads = [
        pltpu.make_async_copy(kept.at[i], held.at[i], load_sem.at[i]) for i in (2, 0, 1, 3)
    ]
    for load in loads:
        load.start()
    loads[0].wait()
    turn(held.at[2], s_rows)
    place_half(held.at[2], summed, 1 - soon)
    loads[2].wait()
    place_half(held.at[1], summed, soon)
    stores = store_columns(summed, sigma, sigma_sem)
    loads[1].wait()
    dyson_rows(held.at[0], s_rows, r_rows, x_rows)
    loads[3].wait()
    place_half(held.at[3], final, soon)
    turn(s_rows, turned)
    place_half(turned, final, 1 - soon)
    stores += store_columns(final, after, after_sem)
    for store in stores:
        store.wait()


def dyson(kept):
    whole = pl.BlockSpec(memory_space=pltpu.HBM)
    half = pltpu.VMEM((512, 128), F32)
    return pl.pallas_call(
        dyson_kernel,
        out_shape=[jax.ShapeDtypeStruct((256, 512), F32)] * 2,
        in_specs=[whole],
        out_specs=[whole] * 2,
        scratch_shapes=[pltpu.VMEM((4, 512, 128), F32), half]
        + [pltpu.VMEM((1024, 128), F32)] * 2
        + [half] * 3
        + [pltpu.SemaphoreType.DMA((4,))] * 3,
        compiler_params=pltpu.CompilerParams(vmem_limit_bytes=56 * 1024 * 1024),
        cost_estimate=pl.CostEstimate(
            flops=3 * 10**7, bytes_accessed=2 * 10**6, transcendentals=0
        ),
    )(kept)


def body(green, phonon, lag_offsets, grad_table, neighbor_grad):
    own = green.reshape(256, 512)
    kept = scatter(own, phonon, lag_offsets.reshape(1, 32), grad_table, neighbor_grad)
    sigma, after = dyson(kept)
    return sigma.reshape(green.shape), after.reshape(green.shape)


def solution(mesh):
    whole = P("mom", ("energy", "tile"), None, None)
    rows = P(("energy", "tile"), None)
    return jax.shard_map(
        body,
        mesh=mesh,
        in_specs=(whole, rows, P(), P(), rows),
        out_specs=(whole, whole),
        check_vma=False,
    )
```

```python
import functools

import jax
import jax.numpy as jnp
from jax import lax
from jax.experimental import pallas as pl
from jax.experimental.pallas import tpu as pltpu
from jax.sharding import PartitionSpec as P

MESH = pl.DeviceIdType.MESH
EXACT = lax.Precision.HIGHEST
F32, BF16 = jnp.float32, jnp.bfloat16
NE = 128
PAIRS = 128
NBR = 4


def split(value):
    high = value.astype(BF16)
    return high, (value - high.astype(F32)).astype(BF16)


def iota(shape, dim):
    return lax.broadcasted_iota(jnp.int32, shape, dim)


def coordinates():
    energy = lax.axis_index("energy")
    return (
        energy // 16 + 4 * lax.axis_index("tile"),
        (energy // 4) % 4,
        energy % 4,
        lax.axis_index("mom"),
    )


def device_at(z, y, x):
    return {"energy": (z % 4) * 16 + y * 4 + x, "tile": z // 4}


def flat_at(z, y, x):
    return ((z % 4) * 16 + y * 4 + x) * 2 + z // 4


def neighbours(z, y, x):
    column = [device_at((z + step) % 8, y, x) for step in range(1, 8)]
    plane = [device_at(z, (y + step // 4) % 4, (x + step % 4) % 4) for step in range(1, 16)]
    return column, plane


def signal(sem, device):
    pl.semaphore_signal(sem, inc=1, device_id=device, device_id_type=MESH)


def tile_rows(block):
    return pl.ds(pl.multiple_of(block * 8, 8), 8)


def exchange_start(position, half, source, landing, send_sem, recv_sem):
    z, y, x = position
    here = tile_rows(flat_at(z, y, x))
    depth = [(z + step) % 8 for step in (0, 4, 3, 5, 2, 6, 1, 7)]

    def send(zz, yy, xx):
        pltpu.make_async_remote_copy(
            src_ref=source.at[tile_rows(flat_at(zz, yy, xx))],
            dst_ref=landing.at[here],
            send_sem=send_sem,
            recv_sem=recv_sem,
            device_id=device_at(zz, yy, xx),
            device_id_type=MESH,
        ).start()

    def plane(k):
        yy = (y + 2 + k // 2) % 4
        xx = (x + half + 2 * ((k + 1) % 2)) % 4
        for zz in depth:
            send(zz, yy, xx)

    if half == 0:
        pl.loop(0, 5)(plane)
        pl.loop(6, 8)(plane)
        for zz in depth[1:]:
            send(zz, y, x)
    else:
        pl.loop(0, 8)(plane)

    if half == 0:
        landing[here, :] = source[here, :]


def exchange_descriptor(half, source, landing, send_sem, recv_sem, device):
    rows = pl.ds(0, 8 * (63 + half))
    return pltpu.make_async_remote_copy(
        src_ref=source.at[rows],
        dst_ref=landing.at[rows],
        send_sem=send_sem,
        recv_sem=recv_sem,
        device_id=device,
        device_id_type=MESH,
    )


def build_weights(core, phonon, lags, whi, wlo):
    place = (iota((256, 32), 0) // 4) % 32 == iota((256, 32), 1)
    lag_column = jnp.sum(
        jnp.where(place, jnp.broadcast_to(lags[...], (256, 32)), 0), axis=1, keepdims=True
    )
    lane = iota((256, 256), 1)
    offset = jnp.where(lane < 128, lane, lane - 256)
    picked = jnp.where(offset == -lag_column, 1.0, 0.0).astype(F32)
    row, column = iota((8, 256), 0), iota((8, 256), 1)
    mine = (column // 128 == row // 4) & (column % 4 == row % 4)
    coeffs = jnp.where(mine, jnp.broadcast_to(phonon[pl.ds(core, 1), :], (8, 256)), 0.0)
    profile = jnp.dot(coeffs, picked, precision=EXACT, preferred_element_type=F32)
    source, target = iota((256, 256), 0), iota((256, 256), 1)
    energy = 4 * (target % 32) + 2 * (target // 128) + (target // 32) % 2
    orders = [
        jnp.where(
            (source % 128 == energy) & (source // 128 == (target // 64 + k) % 2), 1.0, 0.0
        ).astype(BF16)
        for k in range(2)
    ]
    for n in range(NBR):
        parts = [
            jnp.concatenate(
                [
                    pltpu.roll(
                        jnp.broadcast_to(profile[q * 4 + n : q * 4 + n + 1, :], (32, 256)),
                        step,
                        1,
                        stride=4,
                        stride_axis=0,
                    )[:, :128]
                    for q in range(2)
                ],
                axis=1,
            )
            for step in range(4)
        ]
        pieces = split(jnp.concatenate(parts, axis=0))
        for piece, kept in zip(pieces, (whi, wlo)):
            for k in range(2):
                moved = jnp.dot(piece, orders[k], preferred_element_type=F32).astype(BF16)
                for s in range(2):
                    rows = slice(s * 128 + k * 64, s * 128 + k * 64 + 64)
                    for other in range(2):
                        kept[other, rows, n * 128 : n * 128 + 128] = moved[
                            s * 64 : s * 64 + 64, other * 128 : other * 128 + 128
                        ]


def build_kron(core, neighbor, grad, khi, klo, factors):
    column = iota((16, 256), 1)
    mine = column % 16 == iota((16, 256), 0)
    source, target = iota((256, 256), 0), iota((256, 256), 1)
    outer = jnp.where(source // 16 == target // 16, 1.0, 0.0).astype(F32)
    inner = jnp.where(source // 16 == target % 16, 1.0, 0.0).astype(F32)
    for n in range(NBR):
        block = jnp.broadcast_to(grad[pl.ds(neighbor[core, n], 1), :], (16, 256))
        factors[n * 16 : n * 16 + 16, :] = jnp.where(mine, block, 0.0)
    left = factors[...]
    first = jnp.dot(left, outer, precision=EXACT, preferred_element_type=F32)
    second = jnp.dot(left, inner, precision=EXACT, preferred_element_type=F32)
    for n in range(NBR):
        for j in range(16):
            row = first[n * 16 + j : n * 16 + j + 1, :]
            high, low = split(row * second[n * 16 : n * 16 + 16, :])
            rows = slice(n * 256 + j * 16, n * 256 + j * 16 + 16)
            khi[rows, :] = high
            klo[rows, :] = low


def three_passes(left, right):
    lh, ll = left
    rh, rl = right
    return jnp.dot(
        jnp.concatenate([lh, lh, ll], axis=1),
        jnp.concatenate([rh, rl, rh], axis=0),
        preferred_element_type=F32,
    )


def energy_rows(s, zh, k, t):
    return pl.ds(16 * s + 8 * zh + 4 * k + t, 32, stride=32)


def sandwich_half(s, got, khi, klo, fhi, flo):
    loaded = [
        jnp.concatenate(
            [
                jnp.concatenate(
                    [got[energy_rows(s, zh, k, 2 * part + side), :] for side in range(2)], axis=1
                )
                for k in range(2)
                for zh in range(2)
            ],
            axis=0,
        )
        for part in range(2)
    ]
    left = split(jnp.concatenate(loaded, axis=0))
    for n in range(NBR):
        rows = slice(n * 256, n * 256 + 256)
        high, low = split(three_passes(left, (khi[rows, :], klo[rows, :])))
        for part in range(2):
            to, cols = slice(n * 128, n * 128 + 128), slice(part * 256, part * 256 + 256)
            fhi[to, cols] = high[part * 128 : part * 128 + 128, :]
            flo[to, cols] = low[part * 128 : part * 128 + 128, :]


def mix_half(rows, s, whi, wlo, fhi, flo):
    return three_passes((whi[s, rows, :], wlo[s, rows, :]), (fhi[...], flo[...]))


def load_columns(source, target, sems):
    loads = [
        pltpu.make_async_copy(
            source.at[:, pl.ds(t * 128, 128)], target.at[pl.ds(t * 256, 256)], sems.at[t]
        )
        for t in range(4)
    ]
    for load in loads:
        load.start()
    return loads


def atom_rows(t, s, zh, parity):
    return pl.ds(t * 256 + 4 * s + 2 * zh + parity, 32, stride=8)


def block_rows(t, zh, parity):
    return pl.ds(pl.multiple_of(t * 128 + zh * 64 + parity * 32, 32), 32)


QUARTERS = [(t, zh, parity) for t in range(4) for zh in range(2) for parity in range(2)]


def pick_half(source, target, s):
    for t, zh, parity in QUARTERS:
        target[block_rows(t, zh, parity), :] = source[atom_rows(t, s, zh, parity), :]


def place_half(source, target, s):
    for t, zh, parity in QUARTERS:
        target[atom_rows(t, s, zh, parity), :] = source[block_rows(t, zh, parity), :]


def turn(source, target):
    for t in range(4):
        rows = slice(t * 128, t * 128 + 128)
        target[rows, :] = source[rows, :].T


def dyson_rows(g_rows, s_rows, r_rows, x_rows):
    complex_rows(r_rows, g_rows, s_rows, None)
    complex_rows(x_rows, r_rows, g_rows, g_rows)
    complex_rows(s_rows, r_rows, x_rows, g_rows)


def scatter_kernel(
    green, phonon_in, lags_in, grad_in, neighbor_in, kept,
    held, phonon, lags, grad, neighbor,
    swap_out, swap_in, late_out, late_in, stage, got, result, back,
    whi, wlo, khi, klo, factors, fhi, flo, partial, summed, early, g_rows, s_rows, r_rows, x_rows,
    send_sems, recv_sems, stage_sem, load_sem, small_sem, keep_sem,
):
    z, y, x, core = coordinates()
    position = (z, y, x)
    parities = (x % 2, 1 - x % 2)
    sibling = {"mom": 1 - core}
    column, plane = neighbours(z, y, x)
    barrier = pltpu.get_barrier_semaphore()
    for device in [sibling] + plane + column:
        signal(barrier, device)
    loads = load_columns(green, held, load_sem)
    smalls = [
        pltpu.make_async_copy(source, target, small_sem.at[i])
        for i, (source, target) in enumerate(
            [(phonon_in, phonon), (lags_in, lags), (grad_in, grad), (neighbor_in, neighbor)]
        )
    ]
    for small in smalls:
        small.start()

    def channel(i):
        return send_sems.at[i], recv_sems.at[i]

    def swap_of(half, source, target, i):
        return pltpu.make_async_remote_copy(
            src_ref=source.at[half],
            dst_ref=target.at[half],
            send_sem=send_sems.at[i + half],
            recv_sem=recv_sems.at[i + half],
            device_id=sibling,
            device_id_type=MESH,
        )

    for load in loads:
        load.wait()
    for half, s in enumerate(parities):
        for zh in range(2):
            for t in range(4):
                swap_out[half, zh * 4 + t] = held[atom_rows(t, s, zh, 1 - core), :]
    pl.semaphore_wait(barrier, 23)

    swaps = [swap_of(half, swap_out, swap_in, 0) for half in range(2)]
    for swap in swaps:
        swap.start()
    for device in column:
        signal(stage_sem, device)
    for t in range(4):
        stage[pl.ds(core * 4 + t, PAIRS, stride=8), :] = held[
            pl.ds(t * 256 + core, PAIRS, stride=2), :
        ]
    pl.semaphore_wait(stage_sem, 7)
    for half, s in enumerate(parities):
        swaps[half].wait()
        for zh in range(2):
            for t in range(4):
                stage[energy_rows(s, zh, 1 - core, t), :] = swap_in[half, zh * 4 + t]
        exchange_start(position, half, stage, got, *channel(2 + half))

    for small in smalls:
        small.wait()
    build_weights(core, phonon, lags, whi, wlo)
    build_kron(core, neighbor, grad, khi, klo, factors)

    def keep(i, source):
        copy = pltpu.make_async_copy(source, kept.at[i], keep_sem.at[i])
        copy.start()
        return copy

    pick_half(held, r_rows, parities[1])
    turn(r_rows, x_rows)
    keeps = [keep(0, x_rows)]
    pick_half(held, s_rows, parities[0])
    turn(s_rows, g_rows)

    exchange_descriptor(0, stage, got, *channel(2), sibling).wait()
    sandwich_half(parities[0], got, khi, klo, fhi, flo)
    for out in range(2):
        rows = slice(out * 128, out * 128 + 128)
        partial[rows, :] = mix_half(rows, parities[0], whi, wlo, fhi, flo)
    exchange_descriptor(1, stage, got, *channel(3), sibling).wait()
    sandwich_half(parities[1], got, khi, klo, fhi, flo)
    for half, s in enumerate(parities):
        rows = pl.ds(pl.multiple_of(s * 128, 128), 128)
        total = partial[rows, :] + mix_half(rows, parities[1], whi, wlo, fhi, flo)
        for k in range(2):
            for zh in range(2):
                first = k * 64 + zh * 32
                for t in range(4):
                    result[energy_rows(s, zh, k, t), :] = total[
                        first : first + 32, t * 128 : t * 128 + 128
                    ]
        exchange_start(position, half, result, back, *channel(4 + half))

    keeps[0].wait()
    for half, s in enumerate(parities):
        exchange_descriptor(half, result, back, *channel(4 + half), sibling).wait()
        for zh in range(2):
            for t in range(4):
                late_out[half, zh * 4 + t] = back[energy_rows(s, zh, 1 - core, t), :]
        swap_back = swap_of(half, late_out, late_in, 6)
        swap_back.start()
        for zh in range(2):
            for t in range(4):
                summed[half, block_rows(t, zh, core), :] = back[energy_rows(s, zh, core, t), :]
        swap_back.wait()
        for zh in range(2):
            for t in range(4):
                summed[half, block_rows(t, zh, 1 - core), :] = late_in[half, zh * 4 + t]
        keeps.append(keep(1 + half, summed.at[half]))
        if half == 0:
            turn(summed.at[0], s_rows)
            dyson_rows(g_rows, s_rows, r_rows, x_rows)
            turn(s_rows, early)
            keeps.append(keep(3, early))
    for copy in keeps[1:]:
        copy.wait()


def scatter(green, phonon, lags, grad, neighbor):
    column = pltpu.VMEM((1024, 128), F32)
    half = pltpu.VMEM((512, 128), F32)
    swapped = pltpu.VMEM((2, 8, 32, 128), F32)
    return pl.pallas_call(
        scatter_kernel,
        out_shape=jax.ShapeDtypeStruct((4, 512, 128), F32),
        in_specs=[pl.BlockSpec(memory_space=pltpu.HBM)] * 5,
        out_specs=pl.BlockSpec(memory_space=pltpu.HBM),
        scratch_shapes=[
            column,
            pltpu.VMEM((2, 256), F32),
            pltpu.VMEM((1, 32), jnp.int32),
            pltpu.VMEM((64, 256), F32),
            pltpu.SMEM((2, 4), jnp.int32),
            swapped,
            swapped,
            swapped,
            swapped,
            column,
            column,
            column,
            column,
            pltpu.VMEM((2, 256, 512), BF16),
            pltpu.VMEM((2, 256, 512), BF16),
            pltpu.VMEM((1024, 256), BF16),
            pltpu.VMEM((1024, 256), BF16),
            pltpu.VMEM((64, 256), F32),
            pltpu.VMEM((512, 512), BF16),
            pltpu.VMEM((512, 512), BF16),
            pltpu.VMEM((256, 512), F32),
            pltpu.VMEM((2, 512, 128), F32),
            half,
            half,
            half,
            half,
            half,
            pltpu.SemaphoreType.DMA((8,)),
            pltpu.SemaphoreType.DMA((8,)),
            pltpu.SemaphoreType.REGULAR,
            pltpu.SemaphoreType.DMA((4,)),
            pltpu.SemaphoreType.DMA((4,)),
            pltpu.SemaphoreType.DMA((4,)),
        ],
        compiler_params=pltpu.CompilerParams(
            collective_id=0, has_side_effects=True, vmem_limit_bytes=56 * 1024 * 1024
        ),
        cost_estimate=pl.CostEstimate(
            flops=2 * 10**9, bytes_accessed=4 * 10**6, transcendentals=0
        ),
    )(green, phonon, lags, grad, neighbor)


def complex_rows(target, left, right, base):
    @pl.loop(0, 4)
    def _(block):
        first = pl.multiple_of(block * 64, 64)
        real = [None] * 4
        imag = [None] * 4
        for j in range(16):
            b_real = right[j * 16 : j * 16 + 16, :]
            b_imag = right[256 + j * 16 : 256 + j * 16 + 16, :]
            for i in range(4):
                a_real = left[pl.ds(first + i * 16 + j, 1), :]
                a_imag = left[pl.ds(256 + first + i * 16 + j, 1), :]
                add_real = a_real * b_real - a_imag * b_imag
                add_imag = a_real * b_imag + a_imag * b_real
                real[i] = add_real if j == 0 else real[i] + add_real
                imag[i] = add_imag if j == 0 else imag[i] + add_imag
        for i in range(4):
            rows = pl.ds(first + i * 16, 16)
            late = pl.ds(256 + first + i * 16, 16)
            if base is None:
                target[rows, :] = real[i]
                target[late, :] = imag[i]
            else:
                target[rows, :] = base[rows, :] + real[i]
                target[late, :] = base[late, :] + imag[i]


def store_columns(source, target, sems):
    stores = [
        pltpu.make_async_copy(
            source.at[pl.ds(t * 256, 256)], target.at[:, pl.ds(t * 128, 128)], sems.at[t]
        )
        for t in range(4)
    ]
    for store in stores:
        store.start()
    return stores


def dyson_kernel(
    kept, sigma, after, held, turned, summed, final, s_rows, r_rows, x_rows,
    load_sem, sigma_sem, after_sem,
):
    soon = lax.axis_index("energy") % 2
    loads = [
        pltpu.make_async_copy(kept.at[i], held.at[i], load_sem.at[i]) for i in (2, 0, 1, 3)
    ]
    for load in loads:
        load.start()
    loads[0].wait()
    turn(held.at[2], s_rows)
    place_half(held.at[2], summed, 1 - soon)
    loads[2].wait()
    place_half(held.at[1], summed, soon)
    stores = store_columns(summed, sigma, sigma_sem)
    loads[1].wait()
    dyson_rows(held.at[0], s_rows, r_rows, x_rows)
    loads[3].wait()
    place_half(held.at[3], final, soon)
    turn(s_rows, turned)
    place_half(turned, final, 1 - soon)
    stores += store_columns(final, after, after_sem)
    for store in stores:
        store.wait()


def dyson(kept):
    whole = pl.BlockSpec(memory_space=pltpu.HBM)
    half = pltpu.VMEM((512, 128), F32)
    return pl.pallas_call(
        dyson_kernel,
        out_shape=[jax.ShapeDtypeStruct((256, 512), F32)] * 2,
        in_specs=[whole],
        out_specs=[whole] * 2,
        scratch_shapes=[pltpu.VMEM((4, 512, 128), F32), half]
        + [pltpu.VMEM((1024, 128), F32)] * 2
        + [half] * 3
        + [pltpu.SemaphoreType.DMA((4,))] * 3,
        compiler_params=pltpu.CompilerParams(vmem_limit_bytes=56 * 1024 * 1024),
        cost_estimate=pl.CostEstimate(
            flops=3 * 10**7, bytes_accessed=2 * 10**6, transcendentals=0
        ),
    )(kept)


def body(green, phonon, lag_offsets, grad_table, neighbor_grad):
    own = green.reshape(256, 512)
    kept = scatter(own, phonon, lag_offsets.reshape(1, 32), grad_table, neighbor_grad)
    sigma, after = dyson(kept)
    return sigma.reshape(green.shape), after.reshape(green.shape)


def solution(mesh):
    whole = P("mom", ("energy", "tile"), None, None)
    rows = P(("energy", "tile"), None)
    return jax.shard_map(
        body,
        mesh=mesh,
        in_specs=(whole, rows, P(), P(), rows),
        out_specs=(whole, whole),
        check_vma=False,
    )
```

```python
import functools

import jax
import jax.numpy as jnp
from jax import lax
from jax.experimental import pallas as pl
from jax.experimental.pallas import tpu as pltpu
from jax.sharding import PartitionSpec as P

MESH = pl.DeviceIdType.MESH
EXACT = lax.Precision.HIGHEST
F32, BF16 = jnp.float32, jnp.bfloat16
NE = 128
PAIRS = 128
NBR = 4


def split(value):
    high = value.astype(BF16)
    return high, (value - high.astype(F32)).astype(BF16)


def iota(shape, dim):
    return lax.broadcasted_iota(jnp.int32, shape, dim)


def coordinates():
    energy = lax.axis_index("energy")
    return (
        energy // 16 + 4 * lax.axis_index("tile"),
        (energy // 4) % 4,
        energy % 4,
        lax.axis_index("mom"),
    )


def device_at(z, y, x):
    return {"energy": (z % 4) * 16 + y * 4 + x, "tile": z // 4}


def flat_at(z, y, x):
    return ((z % 4) * 16 + y * 4 + x) * 2 + z // 4


def neighbours(z, y, x):
    column = [device_at((z + step) % 8, y, x) for step in range(1, 8)]
    plane = [device_at(z, (y + step // 4) % 4, (x + step % 4) % 4) for step in range(1, 16)]
    return column, plane


def signal(sem, device):
    pl.semaphore_signal(sem, inc=1, device_id=device, device_id_type=MESH)


def tile_rows(block):
    return pl.ds(pl.multiple_of(block * 8, 8), 8)


def exchange_start(position, half, source, landing, send_sem, recv_sem):
    z, y, x = position
    here = tile_rows(flat_at(z, y, x))
    depth = [(z + step) % 8 for step in (0, 4, 3, 5, 2, 6, 1, 7)]

    def send(zz, yy, xx):
        pltpu.make_async_remote_copy(
            src_ref=source.at[tile_rows(flat_at(zz, yy, xx))],
            dst_ref=landing.at[here],
            send_sem=send_sem,
            recv_sem=recv_sem,
            device_id=device_at(zz, yy, xx),
            device_id_type=MESH,
        ).start()

    def plane(k):
        yy = (y + 2 + k // 2) % 4
        xx = (x + half + 2 * ((k + 1) % 2)) % 4
        for zz in depth:
            send(zz, yy, xx)

    if half == 0:
        pl.loop(0, 5)(plane)
        pl.loop(6, 8)(plane)
        for zz in depth[1:]:
            send(zz, y, x)
    else:
        pl.loop(0, 8)(plane)

    if half == 0:
        landing[here, :] = source[here, :]


def exchange_descriptor(half, source, landing, send_sem, recv_sem, device):
    rows = pl.ds(0, 8 * (63 + half))
    return pltpu.make_async_remote_copy(
        src_ref=source.at[rows],
        dst_ref=landing.at[rows],
        send_sem=send_sem,
        recv_sem=recv_sem,
        device_id=device,
        device_id_type=MESH,
    )


def build_weights(core, phonon, lags, whi, wlo):
    place = (iota((256, 32), 0) // 4) % 32 == iota((256, 32), 1)
    lag_column = jnp.sum(
        jnp.where(place, jnp.broadcast_to(lags[...], (256, 32)), 0), axis=1, keepdims=True
    )
    lane = iota((256, 256), 1)
    offset = jnp.where(lane < 128, lane, lane - 256)
    picked = jnp.where(offset == -lag_column, 1.0, 0.0).astype(F32)
    row, column = iota((8, 256), 0), iota((8, 256), 1)
    mine = (column // 128 == row // 4) & (column % 4 == row % 4)
    coeffs = jnp.where(mine, jnp.broadcast_to(phonon[pl.ds(core, 1), :], (8, 256)), 0.0)
    profile = jnp.dot(coeffs, picked, precision=EXACT, preferred_element_type=F32)
    source, target = iota((256, 256), 0), iota((256, 256), 1)
    energy = 4 * (target % 32) + 2 * (target // 128) + (target // 32) % 2
    orders = [
        jnp.where(
            (source % 128 == energy) & (source // 128 == (target // 64 + k) % 2), 1.0, 0.0
        ).astype(BF16)
        for k in range(2)
    ]
    for n in range(NBR):
        parts = [
            jnp.concatenate(
                [
                    pltpu.roll(
                        jnp.broadcast_to(profile[q * 4 + n : q * 4 + n + 1, :], (32, 256)),
                        step,
                        1,
                        stride=4,
                        stride_axis=0,
                    )[:, :128]
                    for q in range(2)
                ],
                axis=1,
            )
            for step in range(4)
        ]
        pieces = split(jnp.concatenate(parts, axis=0))
        for piece, kept in zip(pieces, (whi, wlo)):
            for k in range(2):
                moved = jnp.dot(piece, orders[k], preferred_element_type=F32).astype(BF16)
                for s in range(2):
                    rows = slice(s * 128 + k * 64, s * 128 + k * 64 + 64)
                    for other in range(2):
                        kept[other, rows, n * 128 : n * 128 + 128] = moved[
                            s * 64 : s * 64 + 64, other * 128 : other * 128 + 128
                        ]


def build_kron(core, neighbor, grad, khi, klo, factors):
    column = iota((16, 256), 1)
    mine = column % 16 == iota((16, 256), 0)
    source, target = iota((256, 256), 0), iota((256, 256), 1)
    outer = jnp.where(source // 16 == target // 16, 1.0, 0.0).astype(F32)
    inner = jnp.where(source // 16 == target % 16, 1.0, 0.0).astype(F32)
    for n in range(NBR):
        block = jnp.broadcast_to(grad[pl.ds(neighbor[core, n], 1), :], (16, 256))
        factors[n * 16 : n * 16 + 16, :] = jnp.where(mine, block, 0.0)
    left = factors[...]
    first = jnp.dot(left, outer, precision=EXACT, preferred_element_type=F32)
    second = jnp.dot(left, inner, precision=EXACT, preferred_element_type=F32)
    for n in range(NBR):
        for j in range(16):
            row = first[n * 16 + j : n * 16 + j + 1, :]
            high, low = split(row * second[n * 16 : n * 16 + 16, :])
            rows = slice(n * 256 + j * 16, n * 256 + j * 16 + 16)
            khi[rows, :] = high
            klo[rows, :] = low


def three_passes(left, right):
    lh, ll = left
    rh, rl = right
    return jnp.dot(
        jnp.concatenate([lh, lh, ll], axis=1),
        jnp.concatenate([rh, rl, rh], axis=0),
        preferred_element_type=F32,
    )


def energy_rows(s, zh, k, t):
    return pl.ds(16 * s + 8 * zh + 4 * k + t, 32, stride=32)


def sandwich_half(s, got, khi, klo, fhi, flo):
    loaded = [
        jnp.concatenate(
            [
                jnp.concatenate(
                    [got[energy_rows(s, zh, k, 2 * part + side), :] for side in range(2)], axis=1
                )
                for k in range(2)
                for zh in range(2)
            ],
            axis=0,
        )
        for part in range(2)
    ]
    left = split(jnp.concatenate(loaded, axis=0))
    for n in range(NBR):
        rows = slice(n * 256, n * 256 + 256)
        high, low = split(three_passes(left, (khi[rows, :], klo[rows, :])))
        for part in range(2):
            to, cols = slice(n * 128, n * 128 + 128), slice(part * 256, part * 256 + 256)
            fhi[to, cols] = high[part * 128 : part * 128 + 128, :]
            flo[to, cols] = low[part * 128 : part * 128 + 128, :]


def mix_half(rows, s, whi, wlo, fhi, flo):
    return three_passes((whi[s, rows, :], wlo[s, rows, :]), (fhi[...], flo[...]))


def load_columns(source, target, sems):
    loads = [
        pltpu.make_async_copy(
            source.at[:, pl.ds(t * 128, 128)], target.at[pl.ds(t * 256, 256)], sems.at[t]
        )
        for t in range(4)
    ]
    for load in loads:
        load.start()
    return loads


def atom_rows(t, s, zh, parity):
    return pl.ds(t * 256 + 4 * s + 2 * zh + parity, 32, stride=8)


def block_rows(t, zh, parity):
    return pl.ds(pl.multiple_of(t * 128 + zh * 64 + parity * 32, 32), 32)


QUARTERS = [(t, zh, parity) for t in range(4) for zh in range(2) for parity in range(2)]


def pick_half(source, target, s):
    for t, zh, parity in QUARTERS:
        target[block_rows(t, zh, parity), :] = source[atom_rows(t, s, zh, parity), :]


def place_half(source, target, s):
    for t, zh, parity in QUARTERS:
        target[atom_rows(t, s, zh, parity), :] = source[block_rows(t, zh, parity), :]


def turn(source, target):
    for t in range(4):
        rows = slice(t * 128, t * 128 + 128)
        target[rows, :] = source[rows, :].T


def dyson_rows(g_rows, s_rows, r_rows, x_rows):
    complex_rows(r_rows, g_rows, s_rows, None)
    complex_rows(x_rows, r_rows, g_rows, g_rows)
    complex_rows(s_rows, r_rows, x_rows, g_rows)


def scatter_kernel(
    green, phonon_in, lags_in, grad_in, neighbor_in, kept, late,
    held, phonon, lags, grad, neighbor,
    swap_out, swap_in, late_out, late_in, stage, got, result, back,
    whi, wlo, khi, klo, factors, fhi, flo, partial, summed, early, g_rows, s_rows, r_rows, x_rows,
    send_sems, recv_sems, stage_sem, load_sem, small_sem, keep_sem,
):
    z, y, x, core = coordinates()
    position = (z, y, x)
    parities = (x % 2, 1 - x % 2)
    sibling = {"mom": 1 - core}
    column, plane = neighbours(z, y, x)
    barrier = pltpu.get_barrier_semaphore()
    for device in [sibling] + plane + column:
        signal(barrier, device)
    loads = load_columns(green, held, load_sem)
    smalls = [
        pltpu.make_async_copy(source, target, small_sem.at[i])
        for i, (source, target) in enumerate(
            [(phonon_in, phonon), (lags_in, lags), (grad_in, grad), (neighbor_in, neighbor)]
        )
    ]
    for small in smalls:
        small.start()

    def channel(i):
        return send_sems.at[i], recv_sems.at[i]

    def swap_of(half, source, target, i):
        return pltpu.make_async_remote_copy(
            src_ref=source.at[half],
            dst_ref=target.at[half],
            send_sem=send_sems.at[i + half],
            recv_sem=recv_sems.at[i + half],
            device_id=sibling,
            device_id_type=MESH,
        )

    for load in loads:
        load.wait()
    for half, s in enumerate(parities):
        for zh in range(2):
            for t in range(4):
                swap_out[half, zh * 4 + t] = held[atom_rows(t, s, zh, 1 - core), :]
    pl.semaphore_wait(barrier, 23)

    swaps = [swap_of(half, swap_out, swap_in, 0) for half in range(2)]
    for swap in swaps:
        swap.start()
    for device in column:
        signal(stage_sem, device)
    for t in range(4):
        stage[pl.ds(core * 4 + t, PAIRS, stride=8), :] = held[
            pl.ds(t * 256 + core, PAIRS, stride=2), :
        ]
    pl.semaphore_wait(stage_sem, 7)
    for half, s in enumerate(parities):
        swaps[half].wait()
        for zh in range(2):
            for t in range(4):
                stage[energy_rows(s, zh, 1 - core, t), :] = swap_in[half, zh * 4 + t]
        exchange_start(position, half, stage, got, *channel(2 + half))

    for small in smalls:
        small.wait()
    build_weights(core, phonon, lags, whi, wlo)
    build_kron(core, neighbor, grad, khi, klo, factors)

    def keep(i, source):
        copy = pltpu.make_async_copy(source, kept.at[i], keep_sem.at[i])
        copy.start()
        return copy

    pick_half(held, r_rows, parities[1])
    turn(r_rows, x_rows)
    keeps = [keep(0, x_rows)]
    pick_half(held, s_rows, parities[0])
    turn(s_rows, g_rows)

    exchange_descriptor(0, stage, got, *channel(2), sibling).wait()
    sandwich_half(parities[0], got, khi, klo, fhi, flo)
    for out in range(2):
        rows = slice(out * 128, out * 128 + 128)
        partial[rows, :] = mix_half(rows, parities[0], whi, wlo, fhi, flo)
    exchange_descriptor(1, stage, got, *channel(3), sibling).wait()
    sandwich_half(parities[1], got, khi, klo, fhi, flo)
    for half, s in enumerate(parities):
        rows = pl.ds(pl.multiple_of(s * 128, 128), 128)
        total = partial[rows, :] + mix_half(rows, parities[1], whi, wlo, fhi, flo)
        for k in range(2):
            for zh in range(2):
                first = k * 64 + zh * 32
                for t in range(4):
                    result[energy_rows(s, zh, k, t), :] = total[
                        first : first + 32, t * 128 : t * 128 + 128
                    ]
        exchange_start(position, half, result, back, *channel(4 + half))

    keeps[0].wait()
    for half, s in enumerate(parities):
        exchange_descriptor(half, result, back, *channel(4 + half), sibling).wait()
        for zh in range(2):
            for t in range(4):
                late_out[half, zh * 4 + t] = back[energy_rows(s, zh, 1 - core, t), :]
        if half == 1:
            break
        swap_back = swap_of(half, late_out, late_in, 6)
        swap_back.start()
        for zh in range(2):
            for t in range(4):
                summed[block_rows(t, zh, core), :] = back[energy_rows(s, zh, core, t), :]
        swap_back.wait()
        for zh in range(2):
            for t in range(4):
                summed[block_rows(t, zh, 1 - core), :] = late_in[half, zh * 4 + t]
        keeps.append(keep(1, summed))
        turn(summed, s_rows)
        dyson_rows(g_rows, s_rows, r_rows, x_rows)
        turn(s_rows, early)
        keeps.append(keep(2, early))

    swap_late = pltpu.make_async_remote_copy(
        src_ref=late_out.at[1],
        dst_ref=late.at[core],
        send_sem=send_sems.at[7],
        recv_sem=recv_sems.at[7],
        device_id=sibling,
        device_id_type=MESH,
    )
    swap_late.start()
    for zh in range(2):
        for t in range(4):
            late_in[1, zh * 4 + t] = back[energy_rows(parities[1], zh, core, t), :]
    own_late = pltpu.make_async_copy(late_in.at[1], late.at[core], keep_sem.at[3])
    own_late.start()
    own_late.wait()
    swap_late.wait()
    for copy in keeps[1:]:
        copy.wait()


def scatter(green, phonon, lags, grad, neighbor):
    column = pltpu.VMEM((1024, 128), F32)
    half = pltpu.VMEM((512, 128), F32)
    swapped = pltpu.VMEM((2, 8, 32, 128), F32)
    return pl.pallas_call(
        scatter_kernel,
        out_shape=[
            jax.ShapeDtypeStruct((3, 512, 128), F32),
            jax.ShapeDtypeStruct((2, 8, 32, 128), F32),
        ],
        in_specs=[pl.BlockSpec(memory_space=pltpu.HBM)] * 5,
        out_specs=[pl.BlockSpec(memory_space=pltpu.HBM)] * 2,
        scratch_shapes=[
            column,
            pltpu.VMEM((2, 256), F32),
            pltpu.VMEM((1, 32), jnp.int32),
            pltpu.VMEM((64, 256), F32),
            pltpu.SMEM((2, 4), jnp.int32),
            swapped,
            swapped,
            swapped,
            swapped,
            column,
            column,
            column,
            column,
            pltpu.VMEM((2, 256, 512), BF16),
            pltpu.VMEM((2, 256, 512), BF16),
            pltpu.VMEM((1024, 256), BF16),
            pltpu.VMEM((1024, 256), BF16),
            pltpu.VMEM((64, 256), F32),
            pltpu.VMEM((512, 512), BF16),
            pltpu.VMEM((512, 512), BF16),
            pltpu.VMEM((256, 512), F32),
            half,
            half,
            half,
            half,
            half,
            half,
            pltpu.SemaphoreType.DMA((8,)),
            pltpu.SemaphoreType.DMA((8,)),
            pltpu.SemaphoreType.REGULAR,
            pltpu.SemaphoreType.DMA((4,)),
            pltpu.SemaphoreType.DMA((4,)),
            pltpu.SemaphoreType.DMA((4,)),
        ],
        compiler_params=pltpu.CompilerParams(
            collective_id=0, has_side_effects=True, vmem_limit_bytes=56 * 1024 * 1024
        ),
        cost_estimate=pl.CostEstimate(
            flops=2 * 10**9, bytes_accessed=4 * 10**6, transcendentals=0
        ),
    )(green, phonon, lags, grad, neighbor)


def complex_rows(target, left, right, base):
    @pl.loop(0, 4)
    def _(block):
        first = pl.multiple_of(block * 64, 64)
        real = [None] * 4
        imag = [None] * 4
        for j in range(16):
            b_real = right[j * 16 : j * 16 + 16, :]
            b_imag = right[256 + j * 16 : 256 + j * 16 + 16, :]
            for i in range(4):
                a_real = left[pl.ds(first + i * 16 + j, 1), :]
                a_imag = left[pl.ds(256 + first + i * 16 + j, 1), :]
                add_real = a_real * b_real - a_imag * b_imag
                add_imag = a_real * b_imag + a_imag * b_real
                real[i] = add_real if j == 0 else real[i] + add_real
                imag[i] = add_imag if j == 0 else imag[i] + add_imag
        for i in range(4):
            rows = pl.ds(first + i * 16, 16)
            late = pl.ds(256 + first + i * 16, 16)
            if base is None:
                target[rows, :] = real[i]
                target[late, :] = imag[i]
            else:
                target[rows, :] = base[rows, :] + real[i]
                target[late, :] = base[late, :] + imag[i]


def store_columns(source, target, sems):
    stores = [
        pltpu.make_async_copy(
            source.at[pl.ds(t * 256, 256)], target.at[:, pl.ds(t * 128, 128)], sems.at[t]
        )
        for t in range(4)
    ]
    for store in stores:
        store.start()
    return stores


def dyson_kernel(
    kept, late, sigma, after, held, ended, turned, summed, final, s_rows, r_rows, x_rows,
    load_sem, sigma_sem, after_sem,
):
    soon = lax.axis_index("energy") % 2
    first = pltpu.make_async_copy(late, ended, load_sem.at[3])
    first.start()
    loads = [pltpu.make_async_copy(kept.at[i], held.at[i], load_sem.at[i]) for i in range(3)]
    for load in loads:
        load.start()
    first.wait()
    for t in range(4):
        block = jnp.concatenate(
            [ended[parity, zh * 4 + t] for zh in range(2) for parity in range(2)], axis=0
        )
        s_rows[t * 128 : t * 128 + 128, :] = block.T
    for t, zh, parity in QUARTERS:
        summed[atom_rows(t, 1 - soon, zh, parity), :] = ended[parity, zh * 4 + t]
    loads[1].wait()
    place_half(held.at[1], summed, soon)
    stores = store_columns(summed, sigma, sigma_sem)
    loads[0].wait()
    dyson_rows(held.at[0], s_rows, r_rows, x_rows)
    loads[2].wait()
    place_half(held.at[2], final, soon)
    turn(s_rows, turned)
    place_half(turned, final, 1 - soon)
    stores += store_columns(final, after, after_sem)
    for store in stores:
        store.wait()


def dyson(kept, late):
    whole = pl.BlockSpec(memory_space=pltpu.HBM)
    half = pltpu.VMEM((512, 128), F32)
    return pl.pallas_call(
        dyson_kernel,
        out_shape=[jax.ShapeDtypeStruct((256, 512), F32)] * 2,
        in_specs=[whole] * 2,
        out_specs=[whole] * 2,
        scratch_shapes=[
            pltpu.VMEM((3, 512, 128), F32),
            pltpu.VMEM((2, 8, 32, 128), F32),
            half,
        ]
        + [pltpu.VMEM((1024, 128), F32)] * 2
        + [half] * 3
        + [pltpu.SemaphoreType.DMA((4,))] * 3,
        compiler_params=pltpu.CompilerParams(vmem_limit_bytes=56 * 1024 * 1024),
        cost_estimate=pl.CostEstimate(
            flops=3 * 10**7, bytes_accessed=2 * 10**6, transcendentals=0
        ),
    )(kept, late)


def body(green, phonon, lag_offsets, grad_table, neighbor_grad):
    own = green.reshape(256, 512)
    held = scatter(own, phonon, lag_offsets.reshape(1, 32), grad_table, neighbor_grad)
    sigma, after = dyson(*held)
    return sigma.reshape(green.shape), after.reshape(green.shape)


def solution(mesh):
    whole = P("mom", ("energy", "tile"), None, None)
    rows = P(("energy", "tile"), None)
    return jax.shard_map(
        body,
        mesh=mesh,
        in_specs=(whole, rows, P(), P(), rows),
        out_specs=(whole, whole),
        check_vma=False,
    )
```

```python
import functools

import jax
import jax.numpy as jnp
from jax import lax
from jax.experimental import pallas as pl
from jax.experimental.pallas import tpu as pltpu
from jax.sharding import PartitionSpec as P

MESH = pl.DeviceIdType.MESH
EXACT = lax.Precision.HIGHEST
F32, BF16 = jnp.float32, jnp.bfloat16
NE = 128
PAIRS = 128
NBR = 4


def split(value):
    high = value.astype(BF16)
    return high, (value - high.astype(F32)).astype(BF16)


def iota(shape, dim):
    return lax.broadcasted_iota(jnp.int32, shape, dim)


def coordinates():
    energy = lax.axis_index("energy")
    return (
        energy // 16 + 4 * lax.axis_index("tile"),
        (energy // 4) % 4,
        energy % 4,
        lax.axis_index("mom"),
    )


def device_at(z, y, x):
    return {"energy": (z % 4) * 16 + y * 4 + x, "tile": z // 4}


def flat_at(z, y, x):
    return ((z % 4) * 16 + y * 4 + x) * 2 + z // 4


def neighbours(z, y, x):
    column = [device_at((z + step) % 8, y, x) for step in range(1, 8)]
    plane = [device_at(z, (y + step // 4) % 4, (x + step % 4) % 4) for step in range(1, 16)]
    return column, plane


def signal(sem, device):
    pl.semaphore_signal(sem, inc=1, device_id=device, device_id_type=MESH)


def tile_rows(block):
    return pl.ds(pl.multiple_of(block * 8, 8), 8)


def exchange_start(position, half, source, landing, send_sem, recv_sem):
    z, y, x = position
    here = tile_rows(flat_at(z, y, x))
    depth = [(z + step) % 8 for step in (0, 4, 3, 5, 2, 6, 1, 7)]

    def send(zz, yy, xx):
        pltpu.make_async_remote_copy(
            src_ref=source.at[tile_rows(flat_at(zz, yy, xx))],
            dst_ref=landing.at[here],
            send_sem=send_sem,
            recv_sem=recv_sem,
            device_id=device_at(zz, yy, xx),
            device_id_type=MESH,
        ).start()

    def plane(k):
        yy = (y + 2 + k // 2) % 4
        xx = (x + half + 2 * ((k + 1) % 2)) % 4
        for zz in depth:
            send(zz, yy, xx)

    if half == 0:
        pl.loop(0, 5)(plane)
        pl.loop(6, 8)(plane)
        for zz in depth[1:]:
            send(zz, y, x)
    else:
        pl.loop(0, 8)(plane)

    if half == 0:
        landing[here, :] = source[here, :]


def exchange_descriptor(half, source, landing, send_sem, recv_sem, device):
    rows = pl.ds(0, 8 * (63 + half))
    return pltpu.make_async_remote_copy(
        src_ref=source.at[rows],
        dst_ref=landing.at[rows],
        send_sem=send_sem,
        recv_sem=recv_sem,
        device_id=device,
        device_id_type=MESH,
    )


def build_weights(core, phonon, lags, whi, wlo):
    place = (iota((256, 32), 0) // 4) % 32 == iota((256, 32), 1)
    lag_column = jnp.sum(
        jnp.where(place, jnp.broadcast_to(lags[...], (256, 32)), 0), axis=1, keepdims=True
    )
    lane = iota((256, 256), 1)
    offset = jnp.where(lane < 128, lane, lane - 256)
    picked = jnp.where(offset == -lag_column, 1.0, 0.0).astype(F32)
    row, column = iota((8, 256), 0), iota((8, 256), 1)
    mine = (column // 128 == row // 4) & (column % 4 == row % 4)
    coeffs = jnp.where(mine, jnp.broadcast_to(phonon[pl.ds(core, 1), :], (8, 256)), 0.0)
    profile = jnp.dot(coeffs, picked, precision=EXACT, preferred_element_type=F32)
    source, target = iota((256, 256), 0), iota((256, 256), 1)
    energy = 4 * (target % 32) + 2 * (target // 128) + (target // 32) % 2
    orders = [
        jnp.where(
            (source % 128 == energy) & (source // 128 == (target // 64 + k) % 2), 1.0, 0.0
        ).astype(BF16)
        for k in range(2)
    ]
    for n in range(NBR):
        parts = [
            jnp.concatenate(
                [
                    pltpu.roll(
                        jnp.broadcast_to(profile[q * 4 + n : q * 4 + n + 1, :], (32, 256)),
                        step,
                        1,
                        stride=4,
                        stride_axis=0,
                    )[:, :128]
                    for q in range(2)
                ],
                axis=1,
            )
            for step in range(4)
        ]
        pieces = split(jnp.concatenate(parts, axis=0))
        for piece, kept in zip(pieces, (whi, wlo)):
            for k in range(2):
                moved = jnp.dot(piece, orders[k], preferred_element_type=F32).astype(BF16)
                for s in range(2):
                    rows = slice(s * 128 + k * 64, s * 128 + k * 64 + 64)
                    for other in range(2):
                        kept[other, rows, n * 128 : n * 128 + 128] = moved[
                            s * 64 : s * 64 + 64, other * 128 : other * 128 + 128
                        ]


def build_kron(core, neighbor, grad, khi, klo, factors):
    column = iota((16, 256), 1)
    mine = column % 16 == iota((16, 256), 0)
    source, target = iota((256, 256), 0), iota((256, 256), 1)
    outer = jnp.where(source // 16 == target // 16, 1.0, 0.0).astype(F32)
    inner = jnp.where(source // 16 == target % 16, 1.0, 0.0).astype(F32)
    for n in range(NBR):
        block = jnp.broadcast_to(grad[pl.ds(neighbor[core, n], 1), :], (16, 256))
        factors[n * 16 : n * 16 + 16, :] = jnp.where(mine, block, 0.0)
    left = factors[...]
    first = jnp.dot(left, outer, precision=EXACT, preferred_element_type=F32)
    second = jnp.dot(left, inner, precision=EXACT, preferred_element_type=F32)
    for n in range(NBR):
        for j in range(16):
            row = first[n * 16 + j : n * 16 + j + 1, :]
            high, low = split(row * second[n * 16 : n * 16 + 16, :])
            rows = slice(n * 256 + j * 16, n * 256 + j * 16 + 16)
            khi[rows, :] = high
            klo[rows, :] = low


def three_passes(left, right):
    lh, ll = left
    rh, rl = right
    return jnp.dot(
        jnp.concatenate([lh, lh, ll], axis=1),
        jnp.concatenate([rh, rl, rh], axis=0),
        preferred_element_type=F32,
    )


def energy_rows(s, zh, k, t):
    return pl.ds(16 * s + 8 * zh + 4 * k + t, 32, stride=32)


def sandwich_half(s, got, khi, klo, fhi, flo):
    loaded = [
        jnp.concatenate(
            [
                jnp.concatenate(
                    [got[energy_rows(s, zh, k, 2 * part + side), :] for side in range(2)], axis=1
                )
                for k in range(2)
                for zh in range(2)
            ],
            axis=0,
        )
        for part in range(2)
    ]
    left = split(jnp.concatenate(loaded, axis=0))
    for n in range(NBR):
        rows = slice(n * 256, n * 256 + 256)
        high, low = split(three_passes(left, (khi[rows, :], klo[rows, :])))
        for part in range(2):
            to, cols = slice(n * 128, n * 128 + 128), slice(part * 256, part * 256 + 256)
            fhi[to, cols] = high[part * 128 : part * 128 + 128, :]
            flo[to, cols] = low[part * 128 : part * 128 + 128, :]


def mix_half(rows, s, whi, wlo, fhi, flo):
    return three_passes((whi[s, rows, :], wlo[s, rows, :]), (fhi[...], flo[...]))


def load_columns(source, target, sems):
    loads = [
        pltpu.make_async_copy(
            source.at[:, pl.ds(t * 128, 128)], target.at[pl.ds(t * 256, 256)], sems.at[t]
        )
        for t in range(4)
    ]
    for load in loads:
        load.start()
    return loads


def atom_rows(t, s, zh, parity):
    return pl.ds(t * 256 + 4 * s + 2 * zh + parity, 32, stride=8)


def block_rows(t, zh, parity):
    return pl.ds(pl.multiple_of(t * 128 + zh * 64 + parity * 32, 32), 32)


QUARTERS = [(t, zh, parity) for t in range(4) for zh in range(2) for parity in range(2)]


def pick_half(source, target, s):
    for t, zh, parity in QUARTERS:
        target[block_rows(t, zh, parity), :] = source[atom_rows(t, s, zh, parity), :]


def place_half(source, target, s, tiles=range(4)):
    for t, zh, parity in QUARTERS:
        if t in tiles:
            target[atom_rows(t, s, zh, parity), :] = source[block_rows(t, zh, parity), :]


def turn(source, target, tiles=range(4)):
    for t in tiles:
        rows = slice(t * 128, t * 128 + 128)
        target[rows, :] = source[rows, :].T


def dyson_rows(g_rows, s_rows, r_rows, x_rows):
    complex_rows(r_rows, g_rows, s_rows, None)
    complex_rows(x_rows, r_rows, g_rows, g_rows)
    complex_rows(s_rows, r_rows, x_rows, g_rows)


def scatter_kernel(
    green, phonon_in, lags_in, grad_in, neighbor_in, kept, late,
    held, phonon, lags, grad, neighbor,
    swap_out, swap_in, late_out, late_in, stage, got, result, back,
    whi, wlo, khi, klo, factors, fhi, flo, partial, summed, early, g_rows, s_rows, r_rows, x_rows,
    send_sems, recv_sems, stage_sem, load_sem, small_sem, keep_sem,
):
    z, y, x, core = coordinates()
    position = (z, y, x)
    parities = (x % 2, 1 - x % 2)
    sibling = {"mom": 1 - core}
    column, plane = neighbours(z, y, x)
    barrier = pltpu.get_barrier_semaphore()
    for device in [sibling] + plane + column:
        signal(barrier, device)
    loads = load_columns(green, held, load_sem)
    smalls = [
        pltpu.make_async_copy(source, target, small_sem.at[i])
        for i, (source, target) in enumerate(
            [(phonon_in, phonon), (lags_in, lags), (grad_in, grad), (neighbor_in, neighbor)]
        )
    ]
    for small in smalls:
        small.start()

    def channel(i):
        return send_sems.at[i], recv_sems.at[i]

    def swap_of(half, source, target, i):
        return pltpu.make_async_remote_copy(
            src_ref=source.at[half],
            dst_ref=target.at[half],
            send_sem=send_sems.at[i + half],
            recv_sem=recv_sems.at[i + half],
            device_id=sibling,
            device_id_type=MESH,
        )

    for load in loads:
        load.wait()
    for half, s in enumerate(parities):
        for zh in range(2):
            for t in range(4):
                swap_out[half, zh * 4 + t] = held[atom_rows(t, s, zh, 1 - core), :]
    pl.semaphore_wait(barrier, 23)

    swaps = [swap_of(half, swap_out, swap_in, 0) for half in range(2)]
    for swap in swaps:
        swap.start()
    for device in column:
        signal(stage_sem, device)
    for t in range(4):
        stage[pl.ds(core * 4 + t, PAIRS, stride=8), :] = held[
            pl.ds(t * 256 + core, PAIRS, stride=2), :
        ]
    pl.semaphore_wait(stage_sem, 7)
    for half, s in enumerate(parities):
        swaps[half].wait()
        for zh in range(2):
            for t in range(4):
                stage[energy_rows(s, zh, 1 - core, t), :] = swap_in[half, zh * 4 + t]
        exchange_start(position, half, stage, got, *channel(2 + half))

    for small in smalls:
        small.wait()
    build_weights(core, phonon, lags, whi, wlo)
    build_kron(core, neighbor, grad, khi, klo, factors)

    def keep(i, source):
        copy = pltpu.make_async_copy(source, kept.at[i], keep_sem.at[i])
        copy.start()
        return copy

    pick_half(held, r_rows, parities[1])
    turn(r_rows, x_rows)
    keeps = [keep(0, x_rows)]
    pick_half(held, s_rows, parities[0])
    turn(s_rows, g_rows)

    exchange_descriptor(0, stage, got, *channel(2), sibling).wait()
    sandwich_half(parities[0], got, khi, klo, fhi, flo)
    for out in range(2):
        rows = slice(out * 128, out * 128 + 128)
        partial[rows, :] = mix_half(rows, parities[0], whi, wlo, fhi, flo)
    exchange_descriptor(1, stage, got, *channel(3), sibling).wait()
    sandwich_half(parities[1], got, khi, klo, fhi, flo)
    for half, s in enumerate(parities):
        rows = pl.ds(pl.multiple_of(s * 128, 128), 128)
        total = partial[rows, :] + mix_half(rows, parities[1], whi, wlo, fhi, flo)
        for k in range(2):
            for zh in range(2):
                first = k * 64 + zh * 32
                for t in range(4):
                    result[energy_rows(s, zh, k, t), :] = total[
                        first : first + 32, t * 128 : t * 128 + 128
                    ]
        exchange_start(position, half, result, back, *channel(4 + half))

    keeps[0].wait()
    for half, s in enumerate(parities):
        exchange_descriptor(half, result, back, *channel(4 + half), sibling).wait()
        for zh in range(2):
            for t in range(4):
                late_out[half, zh * 4 + t] = back[energy_rows(s, zh, 1 - core, t), :]
        if half == 1:
            break
        swap_back = swap_of(half, late_out, late_in, 6)
        swap_back.start()
        for zh in range(2):
            for t in range(4):
                summed[block_rows(t, zh, core), :] = back[energy_rows(s, zh, core, t), :]
        swap_back.wait()
        for zh in range(2):
            for t in range(4):
                summed[block_rows(t, zh, 1 - core), :] = late_in[half, zh * 4 + t]
        keeps.append(keep(1, summed))
        turn(summed, s_rows)
        dyson_rows(g_rows, s_rows, r_rows, x_rows)
        turn(s_rows, early)
        keeps.append(keep(2, early))

    swap_late = pltpu.make_async_remote_copy(
        src_ref=late_out.at[1],
        dst_ref=late.at[core],
        send_sem=send_sems.at[7],
        recv_sem=recv_sems.at[7],
        device_id=sibling,
        device_id_type=MESH,
    )
    swap_late.start()
    for zh in range(2):
        for t in range(4):
            late_in[1, zh * 4 + t] = back[energy_rows(parities[1], zh, core, t), :]
    own_late = pltpu.make_async_copy(late_in.at[1], late.at[core], keep_sem.at[3])
    own_late.start()
    own_late.wait()
    swap_late.wait()
    for copy in keeps[1:]:
        copy.wait()


def scatter(green, phonon, lags, grad, neighbor):
    column = pltpu.VMEM((1024, 128), F32)
    half = pltpu.VMEM((512, 128), F32)
    swapped = pltpu.VMEM((2, 8, 32, 128), F32)
    return pl.pallas_call(
        scatter_kernel,
        out_shape=[
            jax.ShapeDtypeStruct((3, 512, 128), F32),
            jax.ShapeDtypeStruct((2, 8, 32, 128), F32),
        ],
        in_specs=[pl.BlockSpec(memory_space=pltpu.HBM)] * 5,
        out_specs=[pl.BlockSpec(memory_space=pltpu.HBM)] * 2,
        scratch_shapes=[
            column,
            pltpu.VMEM((2, 256), F32),
            pltpu.VMEM((1, 32), jnp.int32),
            pltpu.VMEM((64, 256), F32),
            pltpu.SMEM((2, 4), jnp.int32),
            swapped,
            swapped,
            swapped,
            swapped,
            column,
            column,
            column,
            column,
            pltpu.VMEM((2, 256, 512), BF16),
            pltpu.VMEM((2, 256, 512), BF16),
            pltpu.VMEM((1024, 256), BF16),
            pltpu.VMEM((1024, 256), BF16),
            pltpu.VMEM((64, 256), F32),
            pltpu.VMEM((512, 512), BF16),
            pltpu.VMEM((512, 512), BF16),
            pltpu.VMEM((256, 512), F32),
            half,
            half,
            half,
            half,
            half,
            half,
            pltpu.SemaphoreType.DMA((8,)),
            pltpu.SemaphoreType.DMA((8,)),
            pltpu.SemaphoreType.REGULAR,
            pltpu.SemaphoreType.DMA((4,)),
            pltpu.SemaphoreType.DMA((4,)),
            pltpu.SemaphoreType.DMA((4,)),
        ],
        compiler_params=pltpu.CompilerParams(
            collective_id=0, has_side_effects=True, vmem_limit_bytes=56 * 1024 * 1024
        ),
        cost_estimate=pl.CostEstimate(
            flops=2 * 10**9, bytes_accessed=4 * 10**6, transcendentals=0
        ),
    )(green, phonon, lags, grad, neighbor)


def complex_rows(target, left, right, base, blocks=(0, 4)):
    @pl.loop(*blocks)
    def _(block):
        first = pl.multiple_of(block * 64, 64)
        real = [None] * 4
        imag = [None] * 4
        for j in range(16):
            b_real = right[j * 16 : j * 16 + 16, :]
            b_imag = right[256 + j * 16 : 256 + j * 16 + 16, :]
            for i in range(4):
                a_real = left[pl.ds(first + i * 16 + j, 1), :]
                a_imag = left[pl.ds(256 + first + i * 16 + j, 1), :]
                add_real = a_real * b_real - a_imag * b_imag
                add_imag = a_real * b_imag + a_imag * b_real
                real[i] = add_real if j == 0 else real[i] + add_real
                imag[i] = add_imag if j == 0 else imag[i] + add_imag
        for i in range(4):
            rows = pl.ds(first + i * 16, 16)
            late = pl.ds(256 + first + i * 16, 16)
            if base is None:
                target[rows, :] = real[i]
                target[late, :] = imag[i]
            else:
                target[rows, :] = base[rows, :] + real[i]
                target[late, :] = base[late, :] + imag[i]


def store_columns(source, target, sems, tiles=range(4)):
    stores = [
        pltpu.make_async_copy(
            source.at[pl.ds(t * 256, 256)], target.at[:, pl.ds(t * 128, 128)], sems.at[t]
        )
        for t in tiles
    ]
    for store in stores:
        store.start()
    return stores


def dyson_kernel(
    kept, late, sigma, after, held, ended, turned, summed, final, s_rows, r_rows, x_rows,
    load_sem, sigma_sem, after_sem,
):
    soon = lax.axis_index("energy") % 2
    first = pltpu.make_async_copy(late, ended, load_sem.at[3])
    first.start()
    loads = [pltpu.make_async_copy(kept.at[i], held.at[i], load_sem.at[i]) for i in range(3)]
    for load in loads:
        load.start()
    first.wait()
    for t in range(4):
        block = jnp.concatenate(
            [ended[parity, zh * 4 + t] for zh in range(2) for parity in range(2)], axis=0
        )
        s_rows[t * 128 : t * 128 + 128, :] = block.T
    for t, zh, parity in QUARTERS:
        summed[atom_rows(t, 1 - soon, zh, parity), :] = ended[parity, zh * 4 + t]
    loads[1].wait()
    place_half(held.at[1], summed, soon)
    stores = store_columns(summed, sigma, sigma_sem)
    loads[0].wait()
    g_rows = held.at[0]
    complex_rows(r_rows, g_rows, s_rows, None)
    complex_rows(x_rows, r_rows, g_rows, g_rows)
    loads[2].wait()
    place_half(held.at[2], final, soon)
    for i in range(2):
        complex_rows(s_rows, r_rows, x_rows, g_rows, (2 * i, 2 * i + 2))
        turn(s_rows, turned, (i, i + 2))
        place_half(turned, final, 1 - soon, (i, i + 2))
        stores += store_columns(final, after, after_sem, (i, i + 2))
    for store in stores:
        store.wait()


def dyson(kept, late):
    whole = pl.BlockSpec(memory_space=pltpu.HBM)
    half = pltpu.VMEM((512, 128), F32)
    return pl.pallas_call(
        dyson_kernel,
        out_shape=[jax.ShapeDtypeStruct((256, 512), F32)] * 2,
        in_specs=[whole] * 2,
        out_specs=[whole] * 2,
        scratch_shapes=[
            pltpu.VMEM((3, 512, 128), F32),
            pltpu.VMEM((2, 8, 32, 128), F32),
            half,
        ]
        + [pltpu.VMEM((1024, 128), F32)] * 2
        + [half] * 3
        + [pltpu.SemaphoreType.DMA((4,))] * 3,
        compiler_params=pltpu.CompilerParams(vmem_limit_bytes=56 * 1024 * 1024),
        cost_estimate=pl.CostEstimate(
            flops=3 * 10**7, bytes_accessed=2 * 10**6, transcendentals=0
        ),
    )(kept, late)


def body(green, phonon, lag_offsets, grad_table, neighbor_grad):
    own = green.reshape(256, 512)
    held = scatter(own, phonon, lag_offsets.reshape(1, 32), grad_table, neighbor_grad)
    sigma, after = dyson(*held)
    return sigma.reshape(green.shape), after.reshape(green.shape)


def solution(mesh):
    whole = P("mom", ("energy", "tile"), None, None)
    rows = P(("energy", "tile"), None)
    return jax.shard_map(
        body,
        mesh=mesh,
        in_specs=(whole, rows, P(), P(), rows),
        out_specs=(whole, whole),
        check_vma=False,
    )
```
